32 devices in a mesh: blk: 2 (over x), head: 4 (over z), bend: 4 (over y, core).
Axes of the slice: x: 2, y: 2, z: 4, core: 2. Of those that a mesh axis runs over, the one named last changes fastest.
Arguments:
- queries: bfloat16 [8192, 768], P(('bend', 'blk', 'head')), parts along dimension 0, may hold values from -9 to 9
- keys_values: bfloat16 [2, 8192, 768], P(None, ('bend', 'blk', 'head')), parts along dimension 1, may hold values from -6 to 6
- surface: bfloat16 [8192, 768], P(('bend', 'blk', 'head')), parts along dimension 0, may hold values from -6 to 6
- out_weight: bfloat16 [768, 768], P('head'), may hold values from -0.21875 to 0.21875
- up_weight: bfloat16 [768, 3072], P('head'), may hold values from -0.21875 to 0.21875
- down_weight: bfloat16 [3072, 768], P('head'), may hold values from -0.109375 to 0.109375
- norm_gain: float32 [768], replicated, may hold values from 0.25 to 1.75
- block_lists: int32 [32, 4], P(('bend', 'blk', 'head')), parts along dimension 0, may hold values from 0 to 7, as said below
- list_lengths: int32 [32], P(('bend', 'blk', 'head')), parts along dimension 0, may hold values from 1 to 4
Outputs:
- mixed_out: bfloat16 [8192, 768], P(('bend', 'blk', 'head')), parts along dimension 0
The draws below stay inside these ranges and needn't reach their ends.
There are 4 independent parts, one for each index of `bend`. The reference program is written for one: setup_inputs(seed, part) draws one part's arguments, and reference() takes and returns one part's arrays. A program takes and returns all parts, laid end to end along the dimension named above; an argument that names none is the same for every part. Nothing has to cross between parts.
Inputs may be any that keep to these rules, and one draw needn't show every extreme that they name: `block_lists`: the list of query block b holds distinct anchor blocks, all within cycle distance 3 (modulo 8) of anchor block b, and its first entry is that block itself.
All inputs are finite; a program needn't handle non-finite values.
Results may differ from the reference program's by a relative error of at most 0.0065.
Values may be sent and summed in bfloat16 or wider, within the bound.
No kernel may reach another device: no remote copies, remote signals or barrier semaphores. Data moves between devices by JAX's collectives and lax.ppermute only.
A program may use at most 128 MiB of HBM per device.

```python
import jax
import jax.numpy as jnp
from jax import lax

D = 768
HEADS = 12
HD = 64
FF = 3072
BLOCK = 256
LIST = 4
QB_DEV = 1
ANCHOR_BLOCKS = 8
REACH = 3
NQB = 8
NQ = 2048
NA = 2048


def draw_queries(key, part):
    drawn_key = jax.random.fold_in(key, 21)
    drawn = jnp.clip(jax.random.normal(drawn_key, (NQ, D), jnp.float32), -6.0, 6.0)
    return drawn.astype(jnp.bfloat16)


def draw_keys_values(key, part):
    drawn_key = jax.random.fold_in(key, 31)
    drawn = jnp.clip(jax.random.normal(drawn_key, (2, NA, D), jnp.float32), -6.0, 6.0)
    return drawn.astype(jnp.bfloat16)


def draw_block_lists(key, part):
    drawn_key = jax.random.fold_in(key, 41)
    candidates = 2 * REACH
    tickets = jax.random.randint(drawn_key, (NQB, candidates), 0, 2 ** 20) * candidates + jnp.arange(candidates)[None, :]
    picked = jnp.argsort(tickets, axis=1)[:, :LIST - 1]
    offsets = jnp.where(picked < REACH, picked - REACH, picked - REACH + 1)
    home_block = jnp.arange(NQB) // QB_DEV
    others = (home_block[:, None] + offsets) % ANCHOR_BLOCKS
    return jnp.concatenate([home_block[:, None], others], axis=1).astype(jnp.int32)


def draw_list_lengths(key, part):
    drawn_key = jax.random.fold_in(key, 51)
    lengths = jax.random.randint(drawn_key, (NQB,), 1, LIST + 1)
    return lengths.at[0].set(LIST).at[1].set(1).astype(jnp.int32)


def level_of(own_key, extent, shards, smallest, high):
    loudness, own = 1.0, jax.random.fold_in(own_key, 6)
    for dim, blocks in shards:
        steps = jnp.exp(jax.random.uniform(jax.random.fold_in(own, dim), (blocks,), jnp.float32, smallest / len(shards), high / len(shards)))
        loudness = loudness * jnp.repeat(steps, extent[dim] // blocks).reshape([-1 if axis == dim else 1 for axis in range(len(extent))])
    return loudness


def centred(key, dims, width, reach, pieces=(), kind=jnp.bfloat16):
    values = jax.random.normal(key, dims, jnp.float32) * width
    if len(pieces) > 0:
        values = level_of(key, dims, pieces, -0.22, 0.18) * values
    return jnp.clip(values, min=-reach, max=reach).astype(kind)


def setup_inputs(seed: int = 0, part: int = 0) -> dict:
    key_list = jax.random.split(jax.random.key(seed), 10)
    part_splits = jax.random.split(jax.random.fold_in(key_list[9], part), 10)
    return {
        "queries": draw_queries(jax.random.fold_in(jax.random.fold_in(key_list[9], part), 71), part),
        "keys_values": draw_keys_values(jax.random.fold_in(jax.random.fold_in(key_list[9], part), 71), part),
        "surface": centred(part_splits[2], (NQ, D), 1.0, 6.0, ((0, 8),)),
        "out_weight": centred(key_list[3], (D, D), D ** -0.5, 0.21875, ((0, 4),)),
        "up_weight": centred(key_list[4], (D, FF), D ** -0.5, 0.21875, ((0, 4),)),
        "down_weight": centred(key_list[5], (FF, D), FF ** -0.5, 0.109375, ((0, 4),)),
        "norm_gain": jnp.clip(1.0 + 0.15 * jax.random.normal(key_list[6], (D,), jnp.float32), 0.25, 1.75),
        "block_lists": draw_block_lists(jax.random.fold_in(jax.random.fold_in(key_list[9], part), 71), part),
        "list_lengths": draw_list_lengths(jax.random.fold_in(jax.random.fold_in(key_list[9], part), 71), part),
    }


def reference(queries, keys_values, surface, out_weight, up_weight, down_weight, norm_gain, block_lists, list_lengths):
    anchor_keys = keys_values[0].reshape(ANCHOR_BLOCKS, BLOCK, HEADS, HD)
    anchor_values = keys_values[1].reshape(ANCHOR_BLOCKS, BLOCK, HEADS, HD)
    query_blocks = queries.reshape(NQB, BLOCK, HEADS, HD)

    def one_block(inputs):
        query_block, anchor_ids, live_count = inputs
        picked_keys = anchor_keys[anchor_ids].astype(jnp.float32)
        picked_values = anchor_values[anchor_ids].astype(jnp.float32)
        scores = jnp.einsum('qhd,lkhd->hqlk', query_block.astype(jnp.float32), picked_keys) * (1.0 / HD ** 0.5)
        live_mask = jnp.arange(LIST, dtype=jnp.int32) < live_count
        scores = jnp.where(live_mask[None, None, :, None], scores, -jnp.inf)
        row_max = lax.optimization_barrier(jnp.max(scores, axis=(2, 3), keepdims=True))
        weights_exp = jnp.exp(scores - row_max)
        row_total = lax.optimization_barrier(jnp.sum(weights_exp, axis=(2, 3)))
        probs = weights_exp.astype(jnp.bfloat16)
        context = jnp.einsum('hqlk,lkhd->qhd', probs.astype(jnp.float32), picked_values)
        context = context / jnp.transpose(row_total)[:, :, None]
        return context.reshape(BLOCK, D).astype(jnp.bfloat16)
    context = lax.map(one_block, (query_blocks, block_lists, list_lengths)).reshape(NQ, D)
    hidden = surface.astype(jnp.float32) + jnp.dot(context, out_weight, preferred_element_type=jnp.float32)
    mean_square = lax.optimization_barrier(jnp.mean(hidden * hidden, axis=1, keepdims=True))
    normed = (hidden * lax.rsqrt(mean_square + 1e-05) * norm_gain[None, :]).astype(jnp.bfloat16)
    activated = jax.nn.gelu(jnp.dot(normed, up_weight, preferred_element_type=jnp.float32), approximate=True).astype(jnp.bfloat16)
    mixed_out = hidden + jnp.dot(activated, down_weight, preferred_element_type=jnp.float32)
    return mixed_out.astype(jnp.bfloat16)
```

```python
import functools
import itertools

import jax
import jax.numpy as jnp
from jax import lax
from jax.experimental import pallas as pl
from jax.experimental.pallas import tpu as pltpu
from jax.sharding import Mesh
from jax.sharding import PartitionSpec as P

HEADS = 12
HD = 64
LIST = 4
MIB = 1024 * 1024
LOG2E = 1.4426950408889634


def passed_along(block, axis, distance):
    devices = range(lax.axis_size(axis))
    route = [((i - distance) % len(devices), i) for i in devices]
    return lax.ppermute(block, axis, route)


def fold_rows(running, left_side, portion):
    return running + jnp.dot(left_side, portion, preferred_element_type=jnp.float32)


def ring_shards(
    queries,
    keys_values,
    surface,
    out_weight,
    up_weight,
    down_weight,
    norm_gain,
    block_lists,
    list_lengths,
):
    row_count, feature_width = queries.shape
    query_blocks = block_lists.shape[0]
    block_rows = row_count // query_blocks
    loop_size = lax.axis_size(("blk", "head"))
    cycle_reach = min(3, (loop_size - 1) // 2)
    own_index = lax.axis_index(("blk", "head"))
    query_heads = queries.reshape(query_blocks, block_rows, HEADS, HD)
    score_scale = 1.0 / HD**0.5
    entry_live = jnp.arange(LIST, dtype=jnp.int32)[None, :] < list_lengths[:, None]
    start_state = (
        jnp.full((query_blocks, HEADS, block_rows), -1e30, jnp.float32),
        jnp.zeros((query_blocks, HEADS, block_rows), jnp.float32),
        jnp.zeros((query_blocks, HEADS, block_rows, HD), jnp.float32),
    )

    def absorb(softmax_state, anchor_pair, source):
        listed = jnp.any((block_lists == source) & entry_live, axis=1)
        running_max, running_sum, running_acc = softmax_state
        block_keys = anchor_pair[0].reshape(block_rows, HEADS, HD)
        block_values = anchor_pair[1].reshape(block_rows, HEADS, HD)
        scores = (
            jnp.einsum(
                "bqhd,khd->bhqk", query_heads, block_keys, preferred_element_type=jnp.float32
            )
            * score_scale
        )
        block_max = jnp.max(scores, axis=3)
        new_max = jnp.where(listed[:, None, None], jnp.maximum(running_max, block_max), running_max)
        ratio = jnp.exp(running_max - new_max)
        weights_exp = jnp.where(
            listed[:, None, None, None], jnp.exp(scores - new_max[..., None]), 0.0
        )
        new_sum = running_sum * ratio + jnp.sum(weights_exp, axis=3)
        probs = weights_exp.astype(jnp.bfloat16)
        new_acc = running_acc * ratio[..., None] + jnp.einsum(
            "bhqk,khd->bhqd", probs, block_values, preferred_element_type=jnp.float32
        )
        return (new_max, new_sum, new_acc)

    moving = passed_along(keys_values, ("blk", "head"), -cycle_reach)
    source = (own_index + cycle_reach) % loop_size
    softmax_state = absorb(start_state, moving, source)
    for cycle_turn in range(2 * cycle_reach):
        moving = passed_along(moving, ("blk", "head"), 1)
        source = (source - 1) % loop_size
        softmax_state = absorb(softmax_state, moving, source)
    final_max, final_sum, final_acc = softmax_state
    context = final_acc / final_sum[..., None]
    context = (
        jnp.transpose(context, (0, 2, 1, 3)).reshape(row_count, feature_width).astype(jnp.bfloat16)
    )
    residual = surface.astype(jnp.float32)
    hidden = fold_rows(residual, context, lax.all_gather(out_weight, "head", axis=0, tiled=True))
    mean_square = jnp.mean(hidden * hidden, axis=1, keepdims=True)
    normed = (hidden * lax.rsqrt(mean_square + 1e-05) * norm_gain[None, :]).astype(jnp.bfloat16)
    up_start = jnp.zeros((row_count, up_weight.shape[1]), jnp.float32)
    pre_gelu = fold_rows(up_start, normed, lax.all_gather(up_weight, "head", axis=0, tiled=True))
    activated = jax.nn.gelu(pre_gelu, approximate=True).astype(jnp.bfloat16)
    mixed_out = fold_rows(
        hidden, activated, lax.all_gather(down_weight, "head", axis=0, tiled=True)
    )
    return mixed_out.astype(jnp.bfloat16)


AXES = ("blk", "head", "side", "core")
SIZES = (2, 4, 2, 2)
DEVICES = list(itertools.product(*(range(size) for size in SIZES)))
ZS = 4
HZ = HEADS // ZS
ANY = pl.BlockSpec(memory_space=pl.ANY)
SMEM = pl.BlockSpec(memory_space=pltpu.SMEM)
VMEM = pl.BlockSpec(memory_space=pltpu.VMEM)


def flat(x, z, y, c):
    return ((x * SIZES[1] + z) * SIZES[2] + y) * SIZES[3] + c


def sent(value, route):
    return lax.ppermute(value, AXES, [(flat(*d), flat(*route(*d))) for d in DEVICES])


def along_head(distance):
    return lambda x, z, y, c: (x, (z + distance) % ZS, y, c)


def over_blk(x, z, y, c):
    return (1 - x, z, y, c)


def plane_first(x, z, y, c):
    return (1 - x, z, y, c) if c == 0 else (x, z, 1 - y, c)


def plane_second(x, z, y, c):
    return (x, z, 1 - y, c) if c == 0 else (1 - x, z, y, c)


def other_core(x, z, y, c):
    return (x, z, y, 1 - c)


def pack_kernel(place, q_ref, kv_ref, out_w, up_w, down_w, *refs):
    kv_slots, q_slots, piece = refs[:ZS], refs[ZS : 2 * ZS], refs[2 * ZS]
    kv_all, q_all, sems = refs[2 * ZS + 1 :]
    x, z, y, c = place[0], place[1], place[2], place[3]
    p = 2 * x + y
    m = 2 * p + c
    ro, cols = out_w.shape[0] // 4, out_w.shape[1] // 2
    ru, rd = up_w.shape[0], down_w.shape[0] // 8
    rows = [ro, ro + ru, ro + ru + rd]
    copies = [
        pltpu.make_async_copy(
            out_w.at[pl.ds(pl.multiple_of(p * ro, 16), ro), pl.ds(pl.multiple_of(c * cols, 128), cols)],
            piece.at[pl.ds(0, ro)],
            sems.at[0],
        ),
        pltpu.make_async_copy(
            up_w.at[:, pl.ds(pl.multiple_of(m * cols, 128), cols)],
            piece.at[pl.ds(rows[0], ru)],
            sems.at[1],
        ),
    ]
    for half in range(2):
        copies.append(
            pltpu.make_async_copy(
                down_w.at[pl.ds(pl.multiple_of(m * rd, 16), rd), pl.ds(half * cols, cols)],
                piece.at[pl.ds(rows[1 + half], rd)],
                sems.at[2 + half],
            )
        )
    for copy in copies:
        copy.start()
    n = q_ref.shape[0] // 2
    for head in range(HEADS):
        lanes = slice(head * HD, (head + 1) * HD)
        kv_all[head // HZ, head % HZ] = jnp.concatenate(
            [kv_ref[0, :, lanes], kv_ref[1, :, lanes]], axis=1
        )
        q_all[head // HZ, head % HZ] = jnp.concatenate([q_ref[:n, lanes], q_ref[n:, lanes]], axis=1)
    for s in range(ZS):
        there = lax.rem(z + s, ZS)
        kv_slots[s][...] = kv_all[there]
        q_slots[s][...] = q_all[there]
    for copy in copies:
        copy.wait()


def packed(place, queries, keys_values, out_weight, up_weight, down_weight):
    rows, width = queries.shape
    cols = width // 2
    piece_rows = out_weight.shape[0] // 4 + up_weight.shape[0] + down_weight.shape[0] // 4
    kv_shape, q_shape = (HZ, rows, 2 * HD), (HZ, rows // 2, 2 * HD)
    made = lambda shape: jax.ShapeDtypeStruct(shape, jnp.bfloat16)
    outs = pl.pallas_call(
        pack_kernel,
        out_shape=[made(kv_shape)] * ZS + [made(q_shape)] * ZS + [made((piece_rows, cols))],
        in_specs=[SMEM, VMEM, VMEM, ANY, ANY, ANY],
        out_specs=[VMEM] * (2 * ZS) + [ANY],
        scratch_shapes=[
            pltpu.VMEM((ZS,) + kv_shape, jnp.bfloat16),
            pltpu.VMEM((ZS,) + q_shape, jnp.bfloat16),
            pltpu.SemaphoreType.DMA((4,)),
        ],
        compiler_params=pltpu.CompilerParams(vmem_limit_bytes=16 * MIB),
        cost_estimate=pl.CostEstimate(flops=0, bytes_accessed=4 * MIB, transcendentals=0),
        name="pack_heads",
    )(place, queries, keys_values, out_weight, up_weight, down_weight)
    return outs[:ZS], outs[ZS : 2 * ZS], outs[2 * ZS]


def attend_kernel(place, lists, *refs):
    kv_near, kv_far, q_slots = refs[:ZS], refs[ZS : 2 * ZS], refs[2 * ZS : 3 * ZS]
    out_slots, (blocks, sems) = refs[3 * ZS : 4 * ZS], refs[4 * ZS :]
    x, z = place[0], place[1]
    copies = []
    for s in range(ZS):
        source = lax.rem(z - s + ZS, ZS)
        for side, held in ((x, kv_near[s]), (1 - x, kv_far[s])):
            copies.append(
                pltpu.make_async_copy(held, blocks.at[side * ZS + source], sems.at[len(copies)])
            )
    for copy in copies:
        copy.start()
    for copy in copies:
        copy.wait()
    n = q_slots[0].shape[1]
    low = lax.broadcasted_iota(jnp.int32, (n, 2 * HD), 1) < HD
    scale = LOG2E / HD**0.5
    for s in range(ZS):

        @pl.loop(0, HZ)
        def _(h, s=s):
            pair = q_slots[s][h]
            results = []
            for half in range(2):
                q = pair if half == 0 else pltpu.roll(pair, HD, 1)
                q = jnp.where(low, q, jnp.zeros_like(q))
                scores = []
                for j in range(LIST):
                    kv = blocks[lists[s, j], h]
                    raw = lax.dot_general(
                        q, kv, (((1,), (1,)), ((), ())), preferred_element_type=jnp.float32
                    )
                    if j > 0:
                        raw = jnp.where(j < lists[s, LIST], raw, -1e30)
                    scores.append(raw)
                top = scores[0]
                for raw in scores[1:]:
                    top = jnp.maximum(top, raw)
                top = jnp.max(top, axis=1, keepdims=True)
                total, acc = None, None
                for j in range(LIST):
                    weights = jnp.exp2((scores[j] - top) * scale)
                    total = weights if j == 0 else total + weights
                    part = jnp.dot(
                        weights.astype(jnp.bfloat16),
                        blocks[lists[s, j], h],
                        preferred_element_type=jnp.float32,
                    )
                    acc = part if j == 0 else acc + part
                results.append(acc / jnp.sum(total, axis=1, keepdims=True))
            upper, lower = results
            both = jnp.where(low, pltpu.roll(upper, HD, 1), lower)
            out_slots[s][h] = both.astype(jnp.bfloat16)


def attended(place, lists, kv_near, kv_far, q_slots):
    kv_shape, q_shape = kv_near[0].shape, q_slots[0].shape
    return pl.pallas_call(
        attend_kernel,
        out_shape=[jax.ShapeDtypeStruct(q_shape, jnp.bfloat16)] * ZS,
        in_specs=[SMEM, SMEM] + [ANY] * (2 * ZS) + [VMEM] * ZS,
        out_specs=[VMEM] * ZS,
        scratch_shapes=[
            pltpu.VMEM((2 * ZS,) + kv_shape, jnp.bfloat16),
            pltpu.SemaphoreType.DMA((2 * ZS,)),
        ],
        compiler_params=pltpu.CompilerParams(vmem_limit_bytes=16 * MIB),
        cost_estimate=pl.CostEstimate(
            flops=2 * 10**9, bytes_accessed=3 * MIB, transcendentals=3 * 10**6
        ),
        name="attend",
    )(place, lists, *kv_near, *kv_far, *q_slots)


def feed_kernel(groups, place, gain, surface, *refs):
    ctx_slots, (out_w, up_w, down_w) = refs[:ZS], refs[ZS : ZS + 3]
    refs = refs[ZS + 3 :]
    count = 2 * 2 * len(groups)
    held, o_ref = refs[:count], refs[count]
    out_all, up_all, down_all, sems = refs[count + 1 :]
    x, z, y, c = place[0], place[1], place[2], place[3]
    rs, width = out_w.shape
    cols = width // 2
    ro, ru, rd = rs // 4, up_w.shape[0], down_w.shape[0] // 8
    rows = [0, ro, ro + ru, ro + ru + rd]
    first, second, third = [], [], []

    def copied(into, source, target, sem):
        into.append(pltpu.make_async_copy(source, target, sems.at[sem]))

    copied(first, out_w, out_all.at[pl.ds(0, rs)], 0)
    copied(second, up_w, up_all.at[pl.ds(pl.multiple_of(z * ru, 16), ru)], 1)
    copied(third, down_w, down_all.at[pl.ds(pl.multiple_of(z * 8 * rd, 16), 8 * rd)], 2)
    at = 0
    for slots in groups:
        for swapped in range(2):
            core = c if swapped == 0 else 1 - c
            fx, fy = jnp.where(core == 0, 1 - x, x), jnp.where(core == 0, y, 1 - y)
            for later in range(2):
                ref = held[at]
                at += 1
                for i, k in enumerate(slots):
                    source = lax.rem(z - k + ZS, ZS)
                    for e in range(2):
                        px, py = (x, y) if e == 0 else (fx, fy)
                        if later:
                            px = jnp.where(core == 0, px, 1 - px)
                            py = jnp.where(core == 0, 1 - py, py)
                        p = 2 * px + py
                        m = 2 * p + core
                        piece = ref.at[e, i]
                        slot_row = ((ZS - k) % ZS) * rs
                        copied(
                            first,
                            piece.at[pl.ds(0, ro)],
                            out_all.at[
                                pl.ds(pl.multiple_of(slot_row + p * ro, 16), ro),
                                pl.ds(pl.multiple_of(core * cols, 128), cols),
                            ],
                            0,
                        )
                        copied(
                            second,
                            piece.at[pl.ds(rows[1], ru)],
                            up_all.at[
                                pl.ds(pl.multiple_of(source * ru, 16), ru),
                                pl.ds(pl.multiple_of(m * cols, 128), cols),
                            ],
                            1,
                        )
                        for half in range(2):
                            copied(
                                third,
                                piece.at[pl.ds(rows[2 + half], rd)],
                                down_all.at[
                                    pl.ds(pl.multiple_of((source * 8 + m) * rd, 16), rd),
                                    pl.ds(half * cols, cols),
                                ],
                                2,
                            )
    for copy in first + second + third:
        copy.start()

    def context_of(half):
        lanes = slice(half * HD, (half + 1) * HD)
        return jnp.concatenate(
            [ctx_slots[s][h, :, lanes] for s in range(ZS) for h in range(HZ)], axis=1
        )

    context = jnp.concatenate([context_of(0), context_of(1)], axis=0)
    for copy in first:
        copy.wait()
    hidden = surface[...].astype(jnp.float32) + jnp.dot(
        context, out_all[...], preferred_element_type=jnp.float32
    )
    mean_square = jnp.mean(hidden * hidden, axis=1, keepdims=True)
    normed = (hidden * lax.rsqrt(mean_square + 1e-05) * gain[...]).astype(jnp.bfloat16)
    for copy in second:
        copy.wait()
    total = hidden
    steps = up_w.shape[1] // width
    for step in range(steps):
        pre = jnp.dot(
            normed, up_all[:, step * width : (step + 1) * width], preferred_element_type=jnp.float32
        )
        act = jax.nn.gelu(pre, approximate=True).astype(jnp.bfloat16)
        if step == 0:
            for copy in third:
                copy.wait()
        total = total + jnp.dot(
            act, down_all[step * width : (step + 1) * width, :], preferred_element_type=jnp.float32
        )
    o_ref[...] = total.astype(jnp.bfloat16)


def fed(groups, place, gain, surface, ctx_slots, weights, held):
    out_weight, up_weight, down_weight = weights
    width, hidden_units = up_weight.shape[0] * ZS, up_weight.shape[1]
    return pl.pallas_call(
        functools.partial(feed_kernel, groups),
        out_shape=jax.ShapeDtypeStruct(surface.shape, jnp.bfloat16),
        in_specs=[SMEM, VMEM, VMEM] + [VMEM] * ZS + [ANY] * (3 + len(held)),
        out_specs=VMEM,
        scratch_shapes=[
            pltpu.VMEM((width, width), jnp.bfloat16),
            pltpu.VMEM((width, hidden_units), jnp.bfloat16),
            pltpu.VMEM((hidden_units, width), jnp.bfloat16),
            pltpu.SemaphoreType.DMA((3,)),
        ],
        compiler_params=pltpu.CompilerParams(vmem_limit_bytes=40 * MIB),
        cost_estimate=pl.CostEstimate(
            flops=3 * 10**9, bytes_accessed=12 * MIB, transcendentals=10**6
        ),
        name="feed",
    )(place, gain, surface, *ctx_slots, out_weight, up_weight, down_weight, *held)


def split_shards(
    queries,
    keys_values,
    surface,
    out_weight,
    up_weight,
    down_weight,
    norm_gain,
    block_lists,
    list_lengths,
):
    place = jnp.stack([lax.axis_index(axis) for axis in AXES]).astype(jnp.int32)
    entries = jnp.concatenate([block_lists[0], list_lengths, jnp.zeros(3, jnp.int32)])[None, :]
    kv_slots, q_slots, piece = packed(
        place, queries, keys_values, out_weight, up_weight, down_weight
    )
    shifts = (1, 3, 2)
    lists, near, q_got = {0: entries}, {0: kv_slots[0]}, {0: q_slots[0]}
    far = {0: sent(kv_slots[0], over_blk)}
    for s in shifts:
        near[s] = sent(kv_slots[s], along_head(s))
    for s in shifts:
        q_got[s] = sent(q_slots[s], along_head(s))
        lists[s] = sent(entries, along_head(s))
    for s in shifts:
        far[s] = sent(near[s], over_blk)

    groups = ((1, 3), (2,))
    held = []
    for slots in groups:
        mine = jnp.stack([sent(piece, along_head(k)) for k in slots])
        pair = jnp.stack([mine, sent(mine, plane_first)])
        other = sent(pair, plane_second)
        held += [pair, other, sent(pair, other_core), sent(other, other_core)]

    order = range(ZS)
    ctx = attended(
        place,
        jnp.concatenate([lists[s] for s in order]),
        [near[s] for s in order],
        [far[s] for s in order],
        [q_got[s] for s in order],
    )
    ctx_slots = [ctx[0]] + [sent(ctx[s], along_head(-s)) for s in range(1, ZS)]
    weights = (out_weight, up_weight, down_weight)
    return fed(groups, place, norm_gain[None, :], surface, ctx_slots, weights, held)


def solution(mesh):
    sizes = (mesh.shape["blk"], mesh.shape["head"], mesh.shape["bend"])
    if sizes == (2, 4, 4):
        mesh = Mesh(mesh.devices.reshape(SIZES), AXES)
        parts, shards = ("side", "core"), split_shards
    else:
        parts, shards = ("bend",), ring_shards
    rows = parts + ("blk", "head")
    return jax.shard_map(
        shards,
        mesh=mesh,
        in_specs=(
            P(rows, None),
            P(None, rows, None),
            P(rows, None),
            P("head", None),
            P("head", None),
            P("head", None),
            P(),
            P(rows, None),
            P(rows),
        ),
        out_specs=P(rows, None),
        check_vma=False,
    )
```

```python
import functools
import itertools

import jax
import jax.numpy as jnp
from jax import lax
from jax.experimental import pallas as pl
from jax.experimental.pallas import tpu as pltpu
from jax.sharding import Mesh
from jax.sharding import PartitionSpec as P

HEADS = 12
HD = 64
LIST = 4
MIB = 1024 * 1024
LOG2E = 1.4426950408889634


def passed_along(block, axis, distance):
    devices = range(lax.axis_size(axis))
    route = [((i - distance) % len(devices), i) for i in devices]
    return lax.ppermute(block, axis, route)


def fold_rows(running, left_side, portion):
    return running + jnp.dot(left_side, portion, preferred_element_type=jnp.float32)


def ring_shards(
    queries,
    keys_values,
    surface,
    out_weight,
    up_weight,
    down_weight,
    norm_gain,
    block_lists,
    list_lengths,
):
    row_count, feature_width = queries.shape
    query_blocks = block_lists.shape[0]
    block_rows = row_count // query_blocks
    loop_size = lax.axis_size(("blk", "head"))
    cycle_reach = min(3, (loop_size - 1) // 2)
    own_index = lax.axis_index(("blk", "head"))
    query_heads = queries.reshape(query_blocks, block_rows, HEADS, HD)
    score_scale = 1.0 / HD**0.5
    entry_live = jnp.arange(LIST, dtype=jnp.int32)[None, :] < list_lengths[:, None]
    start_state = (
        jnp.full((query_blocks, HEADS, block_rows), -1e30, jnp.float32),
        jnp.zeros((query_blocks, HEADS, block_rows), jnp.float32),
        jnp.zeros((query_blocks, HEADS, block_rows, HD), jnp.float32),
    )

    def absorb(softmax_state, anchor_pair, source):
        listed = jnp.any((block_lists == source) & entry_live, axis=1)
        running_max, running_sum, running_acc = softmax_state
        block_keys = anchor_pair[0].reshape(block_rows, HEADS, HD)
        block_values = anchor_pair[1].reshape(block_rows, HEADS, HD)
        scores = (
            jnp.einsum(
                "bqhd,khd->bhqk", query_heads, block_keys, preferred_element_type=jnp.float32
            )
            * score_scale
        )
        block_max = jnp.max(scores, axis=3)
        new_max = jnp.where(listed[:, None, None], jnp.maximum(running_max, block_max), running_max)
        ratio = jnp.exp(running_max - new_max)
        weights_exp = jnp.where(
            listed[:, None, None, None], jnp.exp(scores - new_max[..., None]), 0.0
        )
        new_sum = running_sum * ratio + jnp.sum(weights_exp, axis=3)
        probs = weights_exp.astype(jnp.bfloat16)
        new_acc = running_acc * ratio[..., None] + jnp.einsum(
            "bhqk,khd->bhqd", probs, block_values, preferred_element_type=jnp.float32
        )
        return (new_max, new_sum, new_acc)

    moving = passed_along(keys_values, ("blk", "head"), -cycle_reach)
    source = (own_index + cycle_reach) % loop_size
    softmax_state = absorb(start_state, moving, source)
    for cycle_turn in range(2 * cycle_reach):
        moving = passed_along(moving, ("blk", "head"), 1)
        source = (source - 1) % loop_size
        softmax_state = absorb(softmax_state, moving, source)
    final_max, final_sum, final_acc = softmax_state
    context = final_acc / final_sum[..., None]
    context = (
        jnp.transpose(context, (0, 2, 1, 3)).reshape(row_count, feature_width).astype(jnp.bfloat16)
    )
    residual = surface.astype(jnp.float32)
    hidden = fold_rows(residual, context, lax.all_gather(out_weight, "head", axis=0, tiled=True))
    mean_square = jnp.mean(hidden * hidden, axis=1, keepdims=True)
    normed = (hidden * lax.rsqrt(mean_square + 1e-05) * norm_gain[None, :]).astype(jnp.bfloat16)
    up_start = jnp.zeros((row_count, up_weight.shape[1]), jnp.float32)
    pre_gelu = fold_rows(up_start, normed, lax.all_gather(up_weight, "head", axis=0, tiled=True))
    activated = jax.nn.gelu(pre_gelu, approximate=True).astype(jnp.bfloat16)
    mixed_out = fold_rows(
        hidden, activated, lax.all_gather(down_weight, "head", axis=0, tiled=True)
    )
    return mixed_out.astype(jnp.bfloat16)


AXES = ("blk", "head", "side", "core")
SIZES = (2, 4, 2, 2)
DEVICES = list(itertools.product(*(range(size) for size in SIZES)))
ZS = 4
HZ = HEADS // ZS
NOTE = 16
ANY = pl.BlockSpec(memory_space=pl.ANY)
SMEM = pl.BlockSpec(memory_space=pltpu.SMEM)
VMEM = pl.BlockSpec(memory_space=pltpu.VMEM)
HBM = pl.BlockSpec(memory_space=pltpu.HBM)


def flat(x, z, y, c):
    return ((x * SIZES[1] + z) * SIZES[2] + y) * SIZES[3] + c


def sent(value, route):
    return lax.ppermute(value, AXES, [(flat(*d), flat(*route(*d))) for d in DEVICES])


def along_head(distance):
    return lambda x, z, y, c: (x, (z + distance) % ZS, y, c)


def both_ways(x, z, y, c):
    return (x, (z + 1) % ZS, y, c) if c == 0 else (x, (z - 1) % ZS, y, c)


def over_blk(x, z, y, c):
    return (1 - x, z, y, c)


def plane_first(x, z, y, c):
    return (1 - x, z, y, c) if c == 0 else (x, z, 1 - y, c)


def plane_second(x, z, y, c):
    return (x, z, 1 - y, c) if c == 0 else (1 - x, z, y, c)


def other_core(x, z, y, c):
    return (x, z, y, 1 - c)


def after(value, *earlier):
    return lax.optimization_barrier((value,) + earlier)[0]


def pack_kernel(place, listed, length, q_hbm, kv_hbm, out_w, up_w, down_w, *refs):
    kv_slots, q_slots, piece = refs[:ZS], refs[ZS : 2 * ZS], refs[2 * ZS]
    kv_all, q_all, q_ref, kv_ref, sems = refs[2 * ZS + 1 :]
    x, z, y = place[0], place[1], place[2]
    p = 2 * x + y
    ro, cols = out_w.shape[0] // 4, out_w.shape[1] // 2
    ru, rd = up_w.shape[0], down_w.shape[0] // 8
    rows = [ro, ro + ru, ro + ru + rd]
    copies = [
        pltpu.make_async_copy(kv_hbm, kv_ref, sems.at[0]),
        pltpu.make_async_copy(q_hbm, q_ref, sems.at[1]),
    ]
    for e in range(2):
        m = 2 * p + e
        copies.append(
            pltpu.make_async_copy(
                out_w.at[pl.ds(pl.multiple_of(p * ro, 16), ro), pl.ds(e * cols, cols)],
                piece.at[e, pl.ds(0, ro)],
                sems.at[2],
            )
        )
        copies.append(
            pltpu.make_async_copy(
                up_w.at[:, pl.ds(pl.multiple_of(m * cols, 128), cols)],
                piece.at[e, pl.ds(rows[0], ru)],
                sems.at[2],
            )
        )
        for half in range(2):
            copies.append(
                pltpu.make_async_copy(
                    down_w.at[pl.ds(pl.multiple_of(m * rd, 16), rd), pl.ds(half * cols, cols)],
                    piece.at[e, pl.ds(rows[1 + half], rd)],
                    sems.at[2],
                )
            )
    for copy in copies:
        copy.start()
    n = q_ref.shape[0] // 2
    lane = lax.broadcasted_iota(jnp.int32, (NOTE, 2 * HD), 1)
    note = jnp.where(lane == LIST, length[0], 0)
    for j in range(LIST):
        note = jnp.where(lane == j, listed[0, j], note)
    note = note.astype(jnp.float32).astype(jnp.bfloat16)
    copies[0].wait()
    for head in range(HEADS):
        lanes = slice(head * HD, (head + 1) * HD)
        kv_all[head // HZ, head % HZ] = jnp.concatenate(
            [kv_ref[0, :, lanes], kv_ref[1, :, lanes]], axis=1
        )
    copies[1].wait()
    for head in range(HEADS):
        lanes = slice(head * HD, (head + 1) * HD)
        q_all[head // HZ, (head % HZ) * n : (head % HZ + 1) * n] = jnp.concatenate(
            [q_ref[:n, lanes], q_ref[n:, lanes]], axis=1
        )
    for s in range(ZS):
        there = lax.rem(z + s, ZS)
        kv_slots[s][...] = kv_all[there]
        q_slots[s][: HZ * n] = q_all[there]
        q_slots[s][HZ * n :] = note
    for copy in copies[2:]:
        copy.wait()


def packed(place, listed, length, queries, keys_values, out_weight, up_weight, down_weight):
    rows, width = queries.shape
    cols = width // 2
    piece_rows = out_weight.shape[0] // 4 + up_weight.shape[0] + down_weight.shape[0] // 4
    kv_shape, q_rows = (HZ, rows, 2 * HD), HZ * rows // 2
    made = lambda shape: jax.ShapeDtypeStruct(shape, jnp.bfloat16)
    outs = pl.pallas_call(
        pack_kernel,
        out_shape=[made(kv_shape)] * ZS + [made((q_rows + NOTE, 2 * HD))] * ZS + [made((2, piece_rows, cols))],
        in_specs=[SMEM] * 3 + [HBM] * 5,
        out_specs=[VMEM] * (2 * ZS + 1),
        scratch_shapes=[
            pltpu.VMEM((ZS,) + kv_shape, jnp.bfloat16),
            pltpu.VMEM((ZS, q_rows, 2 * HD), jnp.bfloat16),
            pltpu.VMEM(queries.shape, jnp.bfloat16),
            pltpu.VMEM(keys_values.shape, jnp.bfloat16),
            pltpu.SemaphoreType.DMA((3,)),
        ],
        compiler_params=pltpu.CompilerParams(vmem_limit_bytes=58 * MIB),
        cost_estimate=pl.CostEstimate(flops=0, bytes_accessed=4 * MIB, transcendentals=0),
        name="pack_heads",
    )(place, listed, length, queries, keys_values, out_weight, up_weight, down_weight)
    return outs[:ZS], outs[ZS : 2 * ZS], outs[2 * ZS]


def attend_kernel(place, *refs):
    held, q_ref, o_ref, blocks = refs[: 2 * ZS], refs[2 * ZS], refs[2 * ZS + 1], refs[2 * ZS + 2]
    x, z = place[0], place[1]
    n = o_ref.shape[1]
    note = q_ref[HZ * n :].astype(jnp.float32)
    row = lax.broadcasted_iota(jnp.int32, note.shape, 0)
    lane = lax.broadcasted_iota(jnp.int32, note.shape, 1)

    def noted(j):
        return jnp.max(jnp.where((row == 0) & (lane == j), note, 0.0)).astype(jnp.int32)

    length = noted(LIST)
    for j in range(LIST):
        block = noted(j)
        side, source = block // ZS, lax.rem(block, ZS)
        at = jnp.where(side == x, 0, ZS) + lax.rem(z - source + ZS, ZS)
        for i in range(2 * ZS):

            @pl.when((at == i) & (j < length))
            def _(i=i, j=j):
                blocks[j] = held[i][...]

    low = lax.broadcasted_iota(jnp.int32, (n, 2 * HD), 1) < HD
    scale = LOG2E / HD**0.5

    def attend(q, h, count):
        scores = [
            lax.dot_general(
                q, blocks[j, h], (((1,), (1,)), ((), ())), preferred_element_type=jnp.float32
            )
            for j in range(count)
        ]
        top = functools.reduce(jnp.maximum, scores)
        top = jnp.max(top, axis=1, keepdims=True)
        total, acc = None, None
        for j in range(count):
            weights = jnp.exp2((scores[j] - top) * scale)
            part = jnp.dot(
                weights.astype(jnp.bfloat16), blocks[j, h], preferred_element_type=jnp.float32
            )
            total = weights if j == 0 else total + weights
            acc = part if j == 0 else acc + part
        return acc / jnp.sum(total, axis=1, keepdims=True)

    for count in range(1, LIST + 1):

        @pl.when(length == count)
        def _(count=count):
            for h in range(HZ):
                pair = q_ref[h * n : (h + 1) * n]
                none = jnp.zeros_like(pair)
                upper = attend(jnp.where(low, pair, none), h, count)
                lower = attend(jnp.where(low, pltpu.roll(pair, HD, 1), none), h, count)
                o_ref[h] = jnp.where(low, pltpu.roll(upper, HD, 1), lower).astype(jnp.bfloat16)


def attended(place, held, q):
    kv_shape = held[0].shape
    return pl.pallas_call(
        attend_kernel,
        out_shape=jax.ShapeDtypeStruct((HZ, kv_shape[1] // 2, 2 * HD), jnp.bfloat16),
        in_specs=[SMEM] + [VMEM] * (2 * ZS + 1),
        out_specs=VMEM,
        scratch_shapes=[pltpu.VMEM((LIST,) + kv_shape, jnp.bfloat16)],
        compiler_params=pltpu.CompilerParams(vmem_limit_bytes=16 * MIB),
        cost_estimate=pl.CostEstimate(
            flops=5 * 10**8, bytes_accessed=MIB, transcendentals=8 * 10**5
        ),
        name="attend",
    )(place, *held, q)


def feed_kernel(place, gain, surface, *refs):
    ctx_slots, (out_w, up_w, down_w) = refs[:ZS], refs[ZS : ZS + 3]
    refs = refs[ZS + 3 :]
    count = 4
    held, o_ref = refs[:count], refs[count]
    out_all, up_all, down_all, sems = refs[count + 1 :]
    x, z, y, c = place[0], place[1], place[2], place[3]
    rs, width = out_w.shape
    cols = width // 2
    ro, ru, rd = rs // 4, up_w.shape[0], down_w.shape[0] // 8
    rows = [0, ro, ro + ru, ro + ru + rd]
    first, second, third = [], [], []

    def copied(into, source, target, sem):
        into.append(pltpu.make_async_copy(source, target, sems.at[sem]))

    copied(first, out_w, out_all.at[pl.ds(0, rs)], 0)
    copied(second, up_w, up_all.at[pl.ds(pl.multiple_of(z * ru, 16), ru)], 1)
    copied(third, down_w, down_all.at[pl.ds(pl.multiple_of(z * 8 * rd, 16), 8 * rd)], 2)
    at = 0
    for split in range(2):
        for swapped in range(2):
            core = c if swapped == 0 else 1 - c
            k = 2 if split else 1 + 2 * core
            source = lax.rem(z - k + ZS, ZS)
            slot_row = lax.rem(ZS - k, ZS) * rs
            fx, fy = jnp.where(core == 0, 1 - x, x), jnp.where(core == 0, y, 1 - y)
            ref = held[at]
            at += 1
            for later in range(2):
                for e in range(2):
                    px, py = (x, y) if e == 0 else (fx, fy)
                    if later:
                        px = jnp.where(core == 0, px, 1 - px)
                        py = jnp.where(core == 0, 1 - py, py)
                    p = 2 * px + py
                    for i in range(1 if split else 2):
                        half = core if split else i
                        m = 2 * p + half
                        piece = ref.at[2 * later + e, i]
                        copied(
                            first,
                            piece.at[pl.ds(0, ro)],
                            out_all.at[
                                pl.ds(pl.multiple_of(slot_row + p * ro, 16), ro),
                                pl.ds(pl.multiple_of(half * cols, 128), cols),
                            ],
                            0,
                        )
                        copied(
                            second,
                            piece.at[pl.ds(rows[1], ru)],
                            up_all.at[
                                pl.ds(pl.multiple_of(source * ru, 16), ru),
                                pl.ds(pl.multiple_of(m * cols, 128), cols),
                            ],
                            1,
                        )
                        for side in range(2):
                            copied(
                                third,
                                piece.at[pl.ds(rows[2 + side], rd)],
                                down_all.at[
                                    pl.ds(pl.multiple_of((source * 8 + m) * rd, 16), rd),
                                    pl.ds(side * cols, cols),
                                ],
                                2,
                            )
    for copy in first + second + third:
        copy.start()

    def context_of(half):
        lanes = slice(half * HD, (half + 1) * HD)
        return jnp.concatenate(
            [ctx_slots[s][h, :, lanes] for s in range(ZS) for h in range(HZ)], axis=1
        )

    context = jnp.concatenate([context_of(0), context_of(1)], axis=0)
    for copy in first:
        copy.wait()
    hidden = surface[...].astype(jnp.float32) + jnp.dot(
        context, out_all[...], preferred_element_type=jnp.float32
    )
    mean_square = jnp.mean(hidden * hidden, axis=1, keepdims=True)
    normed = (hidden * lax.rsqrt(mean_square + 1e-05) * gain[...]).astype(jnp.bfloat16)
    for copy in second:
        copy.wait()
    total = hidden
    steps = up_w.shape[1] // width
    for step in range(steps):
        pre = jnp.dot(
            normed, up_all[:, step * width : (step + 1) * width], preferred_element_type=jnp.float32
        )
        act = jax.nn.gelu(pre, approximate=True).astype(jnp.bfloat16)
        if step == 0:
            for copy in third:
                copy.wait()
        total = total + jnp.dot(
            act, down_all[step * width : (step + 1) * width, :], preferred_element_type=jnp.float32
        )
    o_ref[...] = total.astype(jnp.bfloat16)


def fed(place, gain, surface, ctx_slots, weights, held):
    out_weight, up_weight, down_weight = weights
    width, hidden_units = up_weight.shape[0] * ZS, up_weight.shape[1]
    return pl.pallas_call(
        feed_kernel,
        out_shape=jax.ShapeDtypeStruct(surface.shape, jnp.bfloat16),
        in_specs=[SMEM, VMEM, VMEM] + [VMEM] * ZS + [ANY] * (3 + len(held)),
        out_specs=VMEM,
        scratch_shapes=[
            pltpu.VMEM((width, width), jnp.bfloat16),
            pltpu.VMEM((width, hidden_units), jnp.bfloat16),
            pltpu.VMEM((hidden_units, width), jnp.bfloat16),
            pltpu.SemaphoreType.DMA((3,)),
        ],
        compiler_params=pltpu.CompilerParams(vmem_limit_bytes=40 * MIB),
        cost_estimate=pl.CostEstimate(
            flops=3 * 10**9, bytes_accessed=12 * MIB, transcendentals=10**6
        ),
        name="feed",
    )(place, gain, surface, *ctx_slots, out_weight, up_weight, down_weight, *held)


def split_shards(
    queries,
    keys_values,
    surface,
    out_weight,
    up_weight,
    down_weight,
    norm_gain,
    block_lists,
    list_lengths,
):
    place = jnp.stack([lax.axis_index(axis) for axis in AXES]).astype(jnp.int32)
    kv_slots, q_slots, piece = packed(
        place, block_lists, list_lengths, queries, keys_values, out_weight, up_weight, down_weight
    )
    core = place[3]
    kv_slots, q_slots = list(kv_slots), list(q_slots)
    near, q, far = {0: kv_slots[0]}, {0: q_slots[0]}, {}
    w13 = sent(piece, both_ways)
    far[0] = sent(kv_slots[0], over_blk)
    near[1], near[3] = (sent(kv_slots[s], along_head(s)) for s in (1, 3))
    w13, near[1], near[3], far[0], kv_slots[2] = lax.optimization_barrier(
        (w13, near[1], near[3], far[0], kv_slots[2])
    )
    first13 = sent(w13, plane_first)
    far13 = sent(jnp.stack([near[1], near[3]]), over_blk)
    near[2] = sent(kv_slots[2], along_head(2))
    w2 = sent(lax.dynamic_index_in_dim(w13, core, 0, keepdims=True), both_ways)
    first13, far13, near[2], w2, q_slots[1], q_slots[2], q_slots[3] = lax.optimization_barrier(
        (first13, far13, near[2], w2, q_slots[1], q_slots[2], q_slots[3])
    )
    far[1], far[3] = far13[0], far13[1]
    pair13 = jnp.stack([w13, first13])
    second13 = sent(pair13, plane_second)
    far[2] = sent(near[2], over_blk)
    for s in (2, 1, 3):
        q[s] = sent(q_slots[s], along_head(s))
    first2 = sent(w2, plane_first)
    first2, q[1], q[2], q[3], far[2], second13 = lax.optimization_barrier((first2, q[1], q[2], q[3], far[2], second13))
    pair2 = jnp.stack([w2, first2])
    second2 = sent(pair2, plane_second)
    blocks = [near[s] for s in range(ZS)] + [far[s] for s in range(ZS)]
    ctx_slots, ctxs = {}, []
    for s in (2, 1, 3, 0):
        ctx = attended(place, blocks, q[s])
        ctxs.append(ctx)
        ctx_slots[s] = sent(ctx, along_head(-s)) if s else ctx
    all13 = jnp.concatenate([pair13, second13])
    core13 = sent(all13, other_core)
    all2 = jnp.concatenate([after(pair2, *ctxs[:3]), second2])
    held = [all13, core13, all2, sent(all2, other_core)]
    weights = (out_weight, up_weight, down_weight)
    ctx_slots = [ctx_slots[s] for s in range(ZS)]
    return fed(place, norm_gain[None, :], surface, ctx_slots, weights, held)


def solution(mesh):
    sizes = (mesh.shape["blk"], mesh.shape["head"], mesh.shape["bend"])
    if sizes == (2, 4, 4):
        mesh = Mesh(mesh.devices.reshape(SIZES), AXES)
        parts, shards = ("side", "core"), split_shards
    else:
        parts, shards = ("bend",), ring_shards
    rows = parts + ("blk", "head")
    return jax.shard_map(
        shards,
        mesh=mesh,
        in_specs=(
            P(rows, None),
            P(None, rows, None),
            P(rows, None),
            P("head", None),
            P("head", None),
            P("head", None),
            P(),
            P(rows, None),
            P(rows),
        ),
        out_specs=P(rows, None),
        check_vma=False,
    )
```

```python
import functools
import itertools

import jax
import jax.numpy as jnp
from jax import lax
from jax.experimental import pallas as pl
from jax.experimental.pallas import tpu as pltpu
from jax.sharding import Mesh
from jax.sharding import PartitionSpec as P

HEADS = 12
HD = 64
LIST = 4
MIB = 1024 * 1024
LOG2E = 1.4426950408889634


def passed_along(block, axis, distance):
    devices = range(lax.axis_size(axis))
    route = [((i - distance) % len(devices), i) for i in devices]
    return lax.ppermute(block, axis, route)


def fold_rows(running, left_side, portion):
    return running + jnp.dot(left_side, portion, preferred_element_type=jnp.float32)


def ring_shards(
    queries,
    keys_values,
    surface,
    out_weight,
    up_weight,
    down_weight,
    norm_gain,
    block_lists,
    list_lengths,
):
    row_count, feature_width = queries.shape
    query_blocks = block_lists.shape[0]
    block_rows = row_count // query_blocks
    loop_size = lax.axis_size(("blk", "head"))
    cycle_reach = min(3, (loop_size - 1) // 2)
    own_index = lax.axis_index(("blk", "head"))
    query_heads = queries.reshape(query_blocks, block_rows, HEADS, HD)
    score_scale = 1.0 / HD**0.5
    entry_live = jnp.arange(LIST, dtype=jnp.int32)[None, :] < list_lengths[:, None]
    start_state = (
        jnp.full((query_blocks, HEADS, block_rows), -1e30, jnp.float32),
        jnp.zeros((query_blocks, HEADS, block_rows), jnp.float32),
        jnp.zeros((query_blocks, HEADS, block_rows, HD), jnp.float32),
    )

    def absorb(softmax_state, anchor_pair, source):
        listed = jnp.any((block_lists == source) & entry_live, axis=1)
        running_max, running_sum, running_acc = softmax_state
        block_keys = anchor_pair[0].reshape(block_rows, HEADS, HD)
        block_values = anchor_pair[1].reshape(block_rows, HEADS, HD)
        scores = (
            jnp.einsum(
                "bqhd,khd->bhqk", query_heads, block_keys, preferred_element_type=jnp.float32
            )
            * score_scale
        )
        block_max = jnp.max(scores, axis=3)
        new_max = jnp.where(listed[:, None, None], jnp.maximum(running_max, block_max), running_max)
        ratio = jnp.exp(running_max - new_max)
        weights_exp = jnp.where(
            listed[:, None, None, None], jnp.exp(scores - new_max[..., None]), 0.0
        )
        new_sum = running_sum * ratio + jnp.sum(weights_exp, axis=3)
        probs = weights_exp.astype(jnp.bfloat16)
        new_acc = running_acc * ratio[..., None] + jnp.einsum(
            "bhqk,khd->bhqd", probs, block_values, preferred_element_type=jnp.float32
        )
        return (new_max, new_sum, new_acc)

    moving = passed_along(keys_values, ("blk", "head"), -cycle_reach)
    source = (own_index + cycle_reach) % loop_size
    softmax_state = absorb(start_state, moving, source)
    for cycle_turn in range(2 * cycle_reach):
        moving = passed_along(moving, ("blk", "head"), 1)
        source = (source - 1) % loop_size
        softmax_state = absorb(softmax_state, moving, source)
    final_max, final_sum, final_acc = softmax_state
    context = final_acc / final_sum[..., None]
    context = (
        jnp.transpose(context, (0, 2, 1, 3)).reshape(row_count, feature_width).astype(jnp.bfloat16)
    )
    residual = surface.astype(jnp.float32)
    hidden = fold_rows(residual, context, lax.all_gather(out_weight, "head", axis=0, tiled=True))
    mean_square = jnp.mean(hidden * hidden, axis=1, keepdims=True)
    normed = (hidden * lax.rsqrt(mean_square + 1e-05) * norm_gain[None, :]).astype(jnp.bfloat16)
    up_start = jnp.zeros((row_count, up_weight.shape[1]), jnp.float32)
    pre_gelu = fold_rows(up_start, normed, lax.all_gather(up_weight, "head", axis=0, tiled=True))
    activated = jax.nn.gelu(pre_gelu, approximate=True).astype(jnp.bfloat16)
    mixed_out = fold_rows(
        hidden, activated, lax.all_gather(down_weight, "head", axis=0, tiled=True)
    )
    return mixed_out.astype(jnp.bfloat16)


AXES = ("blk", "head", "side", "core")
SIZES = (2, 4, 2, 2)
DEVICES = list(itertools.product(*(range(size) for size in SIZES)))
ZS = 4
HZ = HEADS // ZS
NOTE = 16
ANY = pl.BlockSpec(memory_space=pl.ANY)
SMEM = pl.BlockSpec(memory_space=pltpu.SMEM)
VMEM = pl.BlockSpec(memory_space=pltpu.VMEM)
HBM = pl.BlockSpec(memory_space=pltpu.HBM)


def flat(x, z, y, c):
    return ((x * SIZES[1] + z) * SIZES[2] + y) * SIZES[3] + c


def sent(value, route):
    return lax.ppermute(value, AXES, [(flat(*d), flat(*route(*d))) for d in DEVICES])


def along_head(distance):
    return lambda x, z, y, c: (x, (z + distance) % ZS, y, c)


def both_ways(x, z, y, c):
    return (x, (z + 1) % ZS, y, c) if c == 0 else (x, (z - 1) % ZS, y, c)


def over_blk(x, z, y, c):
    return (1 - x, z, y, c)


def plane_first(x, z, y, c):
    return (1 - x, z, y, c) if c == 0 else (x, z, 1 - y, c)


def plane_second(x, z, y, c):
    return (x, z, 1 - y, c) if c == 0 else (1 - x, z, y, c)


def other_core(x, z, y, c):
    return (x, z, y, 1 - c)


def after(value, *earlier):
    return lax.optimization_barrier((value,) + earlier)[0]


def pack_kernel(listed_hbm, length_hbm, q_hbm, kv_hbm, out_w, up_w, down_w, *refs):
    kv_slots, q_slots, piece = refs[:ZS], refs[ZS : 2 * ZS], refs[2 * ZS]
    kv_all, q_all, q_ref, kv_ref, listed, length, sems = refs[2 * ZS + 1 :]
    x, z, y = (lax.axis_index(axis) for axis in AXES[:3])
    p = 2 * x + y
    ro, cols = out_w.shape[0] // 4, out_w.shape[1] // 2
    ru, rd = up_w.shape[0], down_w.shape[0] // 8
    rows = [ro, ro + ru, ro + ru + rd]
    copies = [
        pltpu.make_async_copy(kv_hbm, kv_ref, sems.at[0]),
        pltpu.make_async_copy(q_hbm, q_ref, sems.at[1]),
        pltpu.make_async_copy(listed_hbm, listed, sems.at[3]),
        pltpu.make_async_copy(length_hbm, length, sems.at[4]),
    ]
    for e in range(2):
        m = 2 * p + e
        copies.append(
            pltpu.make_async_copy(
                out_w.at[pl.ds(pl.multiple_of(p * ro, 16), ro), pl.ds(e * cols, cols)],
                piece.at[e, pl.ds(0, ro)],
                sems.at[2],
            )
        )
        copies.append(
            pltpu.make_async_copy(
                up_w.at[:, pl.ds(pl.multiple_of(m * cols, 128), cols)],
                piece.at[e, pl.ds(rows[0], ru)],
                sems.at[2],
            )
        )
        for half in range(2):
            copies.append(
                pltpu.make_async_copy(
                    down_w.at[pl.ds(pl.multiple_of(m * rd, 16), rd), pl.ds(half * cols, cols)],
                    piece.at[e, pl.ds(rows[1 + half], rd)],
                    sems.at[2],
                )
            )
    for copy in copies:
        copy.start()
    n = q_ref.shape[0] // 2
    copies[0].wait()
    for pair in range(HEADS // 2):
        lanes = slice(pair * 2 * HD, (pair + 1) * 2 * HD)
        keys, values = kv_ref[0, :, lanes], kv_ref[1, :, lanes]
        even, odd = 2 * pair, 2 * pair + 1
        low = lax.broadcasted_iota(jnp.int32, keys.shape, 1) < HD
        kv_all[even // HZ, even % HZ] = jnp.where(low, keys, pltpu.roll(values, HD, 1))
        kv_all[odd // HZ, odd % HZ] = jnp.where(low, pltpu.roll(keys, HD, 1), values)
    copies[1].wait()
    for pair in range(HEADS // 2):
        lanes = slice(pair * 2 * HD, (pair + 1) * 2 * HD)
        upper, lower = q_ref[:n, lanes], q_ref[n:, lanes]
        even, odd = 2 * pair, 2 * pair + 1
        low = lax.broadcasted_iota(jnp.int32, upper.shape, 1) < HD
        q_all[even // HZ, (even % HZ) * n : (even % HZ + 1) * n] = jnp.where(
            low, upper, pltpu.roll(lower, HD, 1)
        )
        q_all[odd // HZ, (odd % HZ) * n : (odd % HZ + 1) * n] = jnp.where(
            low, pltpu.roll(upper, HD, 1), lower
        )
    copies[2].wait()
    copies[3].wait()
    lane = lax.broadcasted_iota(jnp.int32, (NOTE, 2 * HD), 1)
    note = jnp.where(lane == LIST, length[0], 0)
    for j in range(LIST):
        note = jnp.where(lane == j, listed[0, j], note)
    note = note.astype(jnp.float32).astype(jnp.bfloat16)
    for s in range(ZS):
        there = lax.rem(z + s, ZS)
        kv_slots[s][...] = kv_all[there]
        q_slots[s][: HZ * n] = q_all[there]
        q_slots[s][HZ * n :] = note
    for copy in copies[4:]:
        copy.wait()


def packed(listed, length, queries, keys_values, out_weight, up_weight, down_weight):
    rows, width = queries.shape
    cols = width // 2
    piece_rows = out_weight.shape[0] // 4 + up_weight.shape[0] + down_weight.shape[0] // 4
    kv_shape, q_rows = (HZ, rows, 2 * HD), HZ * rows // 2
    made = lambda shape: jax.ShapeDtypeStruct(shape, jnp.bfloat16)
    outs = pl.pallas_call(
        pack_kernel,
        out_shape=[made(kv_shape)] * ZS + [made((q_rows + NOTE, 2 * HD))] * ZS + [made((2, piece_rows, cols))],
        in_specs=[HBM] * 7,
        out_specs=[VMEM] * (2 * ZS + 1),
        scratch_shapes=[
            pltpu.VMEM((ZS,) + kv_shape, jnp.bfloat16),
            pltpu.VMEM((ZS, q_rows, 2 * HD), jnp.bfloat16),
            pltpu.VMEM(queries.shape, jnp.bfloat16),
            pltpu.VMEM(keys_values.shape, jnp.bfloat16),
            pltpu.SMEM(listed.shape, jnp.int32),
            pltpu.SMEM(length.shape, jnp.int32),
            pltpu.SemaphoreType.DMA((5,)),
        ],
        compiler_params=pltpu.CompilerParams(vmem_limit_bytes=55 * MIB),
        cost_estimate=pl.CostEstimate(flops=0, bytes_accessed=4 * MIB, transcendentals=0),
        name="pack_heads",
    )(listed, length, queries, keys_values, out_weight, up_weight, down_weight)
    return outs[:ZS], outs[ZS : 2 * ZS], outs[2 * ZS]


def attend_kernel(blocks, *refs):
    q_refs, o_refs = refs[: len(refs) // 2], refs[len(refs) // 2 :]
    x, z = (lax.axis_index(axis) for axis in AXES[:2])
    n = o_refs[0].shape[1]
    low = lax.broadcasted_iota(jnp.int32, (n, 2 * HD), 1) < HD
    key_lanes = lax.broadcasted_iota(jnp.int32, (2 * n, 2 * HD), 1) < HD
    scale = LOG2E / HD**0.5
    row = lax.broadcasted_iota(jnp.int32, (NOTE, 2 * HD), 0)
    lane = lax.broadcasted_iota(jnp.int32, (NOTE, 2 * HD), 1)
    digit = jnp.left_shift(1, 3 * jnp.minimum(lane, LIST))
    digit = jnp.where((row == 0) & (lane <= LIST), digit, 0).astype(jnp.float32)
    codes = [
        jnp.sum(q_ref[HZ * n :].astype(jnp.float32) * digit).astype(jnp.int32) for q_ref in q_refs
    ]
    for q_ref, o_ref, code in zip(q_refs, o_refs, codes):
        at = []
        for j in range(LIST):
            block = jnp.bitwise_and(jnp.right_shift(code, 3 * j), 7)
            side, source = block // ZS, lax.rem(block, ZS)
            at.append(jnp.where(side == x, 0, ZS) + lax.rem(z - source + ZS, ZS))
        length = jnp.right_shift(code, 3 * LIST)

        def scored(h, count, q_ref=q_ref, at=at):
            pair = q_ref[h * n : (h + 1) * n]
            none = jnp.zeros_like(pair)
            q = jnp.concatenate(
                [jnp.where(low, pair, none), jnp.where(low, pltpu.roll(pair, HD, 1), none)], axis=0
            )
            scores = [
                lax.dot_general(
                    q, blocks[at[j], h], (((1,), (1,)), ((), ())), preferred_element_type=jnp.float32
                )
                for j in range(count)
            ]
            return scores, jnp.max(functools.reduce(jnp.maximum, scores), axis=1, keepdims=True)

        def summed(h, count, scores, top, o_ref=o_ref, at=at):
            acc = None
            for j in range(count):
                weights = jnp.exp2((scores[j] - top) * scale).astype(jnp.bfloat16)
                values = blocks[at[j], h]
                values = jnp.where(key_lanes, jnp.ones_like(values), values)
                part = jnp.dot(weights, values, preferred_element_type=jnp.float32)
                acc = part if j == 0 else acc + part
            result = acc / pltpu.roll(acc, HD, 1)
            upper, lower = result[:n], result[n:]
            o_ref[h] = jnp.where(low, pltpu.roll(upper, HD, 1), lower).astype(jnp.bfloat16)

        for count in range(1, LIST + 1):

            @pl.when(length == count)
            def _(count=count, scored=scored, summed=summed):
                held = [scored(h, count) for h in range(HZ)]
                for h in range(HZ):
                    summed(h, count, *held[h])


def attended(blocks, queries):
    made = jax.ShapeDtypeStruct((HZ, blocks.shape[2] // 2, 2 * HD), jnp.bfloat16)
    return pl.pallas_call(
        attend_kernel,
        out_shape=[made] * len(queries),
        in_specs=[VMEM] * (1 + len(queries)),
        out_specs=[VMEM] * len(queries),
        compiler_params=pltpu.CompilerParams(vmem_limit_bytes=16 * MIB),
        cost_estimate=pl.CostEstimate(
            flops=5 * 10**8, bytes_accessed=MIB, transcendentals=8 * 10**5
        ),
        name="attend",
    )(blocks, *queries)


def laid(copies, ref, swapped, stage, shapes, into, sems):
    x, z, y, c = (lax.axis_index(axis) for axis in AXES)
    out_all, up_all, down_all = into
    (rs, width), ru, rd = shapes
    cols, ro = width // 2, rs // 4
    rows = [ro, ro + ru, ro + ru + rd]
    core = 1 - c if swapped else c
    first_x, first_y = jnp.where(core == 0, 1 - x, x), jnp.where(core == 0, y, 1 - y)
    second_x, second_y = jnp.where(core == 0, x, 1 - x), jnp.where(core == 0, 1 - y, y)
    mine, far = (x, y), (1 - x, 1 - y)
    first, second = (first_x, first_y), (second_x, second_y)
    near_k = 1 + 2 * core
    if stage == 0:
        pieces = [(near_k, mine, 0), (near_k, mine, 1), (near_k, first, 0), (near_k, first, 1)]
        pieces += [(2, mine, core)]
    elif stage == 1:
        pieces = [(near_k, far, 0), (near_k, far, 1), (near_k, second, 0), (2, first, core)]
    else:
        pieces = [(near_k, second, 1), (2, second, core), (2, far, core)]
    for at, (k, (px, py), half) in enumerate(pieces):
        source = lax.rem(z - k + ZS, ZS)
        slot_row = lax.rem(ZS - k, ZS) * rs
        p = 2 * px + py
        m = 2 * p + half
        piece = ref.at[at]
        copies.append(
            pltpu.make_async_copy(
                piece.at[pl.ds(0, ro)],
                out_all.at[
                    pl.ds(pl.multiple_of(slot_row + p * ro, 16), ro),
                    pl.ds(pl.multiple_of(half * cols, 128), cols),
                ],
                sems.at[0],
            )
        )
        copies.append(
            pltpu.make_async_copy(
                piece.at[pl.ds(rows[0], ru)],
                up_all.at[
                    pl.ds(pl.multiple_of(source * ru, 16), ru),
                    pl.ds(pl.multiple_of(m * cols, 128), cols),
                ],
                sems.at[1],
            )
        )
        for side in range(2):
            copies.append(
                pltpu.make_async_copy(
                    piece.at[pl.ds(rows[1 + side], rd)],
                    down_all.at[
                        pl.ds(pl.multiple_of((source * 8 + m) * rd, 16), rd),
                        pl.ds(side * cols, cols),
                    ],
                    sems.at[2],
                )
            )


def gather_kernel(out_w, up_w, down_w, *refs):
    held, refs = refs[:5], refs[5:]
    out_all, up_all, down_all, sems = refs
    z = lax.axis_index("head")
    rs, ru, rd = out_w.shape[0], up_w.shape[0], down_w.shape[0]
    copies = [
        pltpu.make_async_copy(out_w, out_all.at[pl.ds(0, rs)], sems.at[0]),
        pltpu.make_async_copy(
            up_w, up_all.at[pl.ds(pl.multiple_of(z * ru, 16), ru)], sems.at[1]
        ),
        pltpu.make_async_copy(
            down_w, down_all.at[pl.ds(pl.multiple_of(z * rd, 16), rd)], sems.at[2]
        ),
    ]
    shapes = (out_w.shape, ru, rd // 8)
    for at, ref in enumerate(held):
        laid(copies, ref, at % 2 == 1, at // 2, shapes, refs[:3], sems)
    for copy in copies:
        copy.start()
    for copy in copies:
        copy.wait()


def gathered(out_weight, up_weight, down_weight, *held):
    width, hidden_units = up_weight.shape[0] * ZS, up_weight.shape[1]
    made = lambda *shape: jax.ShapeDtypeStruct(shape, jnp.bfloat16)
    return pl.pallas_call(
        gather_kernel,
        out_shape=[made(width, width), made(width, hidden_units), made(hidden_units, width)],
        in_specs=[ANY] * (3 + len(held)),
        out_specs=[VMEM] * 3,
        scratch_shapes=[pltpu.SemaphoreType.DMA((3,))],
        compiler_params=pltpu.CompilerParams(vmem_limit_bytes=20 * MIB),
        cost_estimate=pl.CostEstimate(flops=0, bytes_accessed=12 * MIB, transcendentals=0),
        name="gather",
    )(out_weight, up_weight, down_weight, *held)


def feed_kernel(gain, surface, *refs):
    ctx_slots, refs = refs[:ZS], refs[ZS + 3 :]
    late_swapped, o_ref, out_all, up_all, down_all, sems = refs
    width, hidden_units = up_all.shape
    copies = []
    shapes = ((width // ZS, width), width // ZS, hidden_units // ZS // 8)
    laid(copies, late_swapped, True, 2, shapes, (out_all, up_all, down_all), sems)
    first = [copies[i] for i in range(len(copies)) if i % 4 == 0]
    second = [copies[i] for i in range(len(copies)) if i % 4 == 1]
    third = [copies[i] for i in range(len(copies)) if i % 4 > 1]
    for copy in first + second + third:
        copy.start()

    tiles = [ctx_slots[s][h] for s in range(ZS) for h in range(HZ)]
    low = lax.broadcasted_iota(jnp.int32, tiles[0].shape, 1) < HD
    upper, lower = [], []
    for left, right in zip(tiles[::2], tiles[1::2]):
        upper.append(jnp.where(low, left, pltpu.roll(right, HD, 1)))
        lower.append(jnp.where(low, pltpu.roll(left, HD, 1), right))
    context = jnp.concatenate(
        [jnp.concatenate(upper, axis=1), jnp.concatenate(lower, axis=1)], axis=0
    )
    for copy in first:
        copy.wait()
    hidden = surface[...].astype(jnp.float32) + jnp.dot(
        context, out_all[...], preferred_element_type=jnp.float32
    )
    mean_square = jnp.mean(hidden * hidden, axis=1, keepdims=True)
    normed = (hidden * lax.rsqrt(mean_square + 1e-05) * gain[...]).astype(jnp.bfloat16)
    for copy in second:
        copy.wait()
    total = hidden
    for step in range(hidden_units // width):
        pre = jnp.dot(
            normed, up_all[:, step * width : (step + 1) * width], preferred_element_type=jnp.float32
        )
        act = jax.nn.gelu(pre, approximate=True).astype(jnp.bfloat16)
        if step == 0:
            for copy in third:
                copy.wait()
        total = total + jnp.dot(
            act, down_all[step * width : (step + 1) * width, :], preferred_element_type=jnp.float32
        )
    o_ref[...] = total.astype(jnp.bfloat16)


def fed(gain, surface, ctx_slots, weights, late_swapped):
    outs = pl.pallas_call(
        feed_kernel,
        out_shape=[jax.ShapeDtypeStruct(v.shape, jnp.bfloat16) for v in (surface, *weights)],
        in_specs=[VMEM, VMEM] + [VMEM] * (ZS + 3) + [ANY],
        out_specs=[VMEM] * 4,
        scratch_shapes=[pltpu.SemaphoreType.DMA((3,))],
        input_output_aliases={2 + ZS: 1, 3 + ZS: 2, 4 + ZS: 3},
        compiler_params=pltpu.CompilerParams(vmem_limit_bytes=30 * MIB),
        cost_estimate=pl.CostEstimate(
            flops=3 * 10**9, bytes_accessed=12 * MIB, transcendentals=10**6
        ),
        name="feed",
    )(gain, surface, *ctx_slots, *weights, late_swapped)
    return outs[0]


def split_shards(
    queries,
    keys_values,
    surface,
    out_weight,
    up_weight,
    down_weight,
    norm_gain,
    block_lists,
    list_lengths,
):
    kv_slots, q_slots, piece = packed(
        block_lists, list_lengths, queries, keys_values, out_weight, up_weight, down_weight
    )
    core = lax.axis_index("core")
    kv_slots, q_slots = list(kv_slots), list(q_slots)
    near, q, far = {0: kv_slots[0]}, {0: q_slots[0]}, {}
    w13 = sent(piece, both_ways)
    far[0] = sent(kv_slots[0], over_blk)
    near[1], near[3] = (sent(kv_slots[s], along_head(s)) for s in (1, 3))
    w13, near[1], near[3], far[0], kv_slots[2] = lax.optimization_barrier(
        (w13, near[1], near[3], far[0], kv_slots[2])
    )
    first13 = sent(w13, plane_first)
    far13 = sent(jnp.stack([near[1], near[3]]), over_blk)
    near[2] = sent(kv_slots[2], along_head(2))
    w2 = sent(lax.dynamic_index_in_dim(w13, core, 0, keepdims=True), both_ways)
    first13, far13, near[2], w2, q_slots[1], q_slots[2], q_slots[3] = lax.optimization_barrier(
        (first13, far13, near[2], w2, q_slots[1], q_slots[2], q_slots[3])
    )
    far[1], far[3] = far13[0], far13[1]
    far[2] = sent(near[2], over_blk)
    away = (2, 1, 3)
    for s in away:
        q[s] = sent(q_slots[s], along_head(s))
    more13 = sent(jnp.concatenate([first13, w13[:1]]), plane_second)
    more2 = sent(lax.dynamic_index_in_dim(first13, core, 0, keepdims=True), both_ways)
    early = jnp.concatenate([w13, first13, w2])
    early_swapped = sent(early, other_core)
    blocks = jnp.stack([near[s] for s in range(ZS)] + [far[s] for s in range(ZS)])
    ctx_slots = dict(zip(away, attended(blocks, [q[s] for s in away])))
    more13, more2 = after(more13, ctx_slots[2], early_swapped), after(more2, ctx_slots[2])
    late = sent(jnp.concatenate([w13[1:], w2, more2]), plane_second)
    for s in away:
        ctx_slots[s] = sent(ctx_slots[s], along_head(-s))
    (ctx_slots[0],) = attended(blocks, [q[0]])
    mid = jnp.concatenate([more13, more2])
    mid_swapped = sent(mid, other_core)
    held = [early, early_swapped, mid, mid_swapped, late]
    late = after(late, ctx_slots[0], ctx_slots[1], ctx_slots[2], ctx_slots[3])
    late_swapped = sent(late, other_core)
    whole = gathered(out_weight, up_weight, down_weight, *held)
    ctx_slots = [ctx_slots[s] for s in range(ZS)]
    return fed(norm_gain[None, :], surface, ctx_slots, whole, late_swapped)


def solution(mesh):
    sizes = (mesh.shape["blk"], mesh.shape["head"], mesh.shape["bend"])
    if sizes == (2, 4, 4):
        mesh = Mesh(mesh.devices.reshape(SIZES), AXES)
        parts, shards = ("side", "core"), split_shards
    else:
        parts, shards = ("bend",), ring_shards
    rows = parts + ("blk", "head")
    return jax.shard_map(
        shards,
        mesh=mesh,
        in_specs=(
            P(rows, None),
            P(None, rows, None),
            P(rows, None),
            P("head", None),
            P("head", None),
            P("head", None),
            P(),
            P(rows, None),
            P(rows),
        ),
        out_specs=P(rows, None),
        check_vma=False,
    )
```

```python
import functools
import itertools

import jax
import jax.numpy as jnp
from jax import lax
from jax.experimental import pallas as pl
from jax.experimental.pallas import tpu as pltpu
from jax.sharding import Mesh
from jax.sharding import PartitionSpec as P

HEADS = 12
HD = 64
LIST = 4
MIB = 1024 * 1024
LOG2E = 1.4426950408889634


def passed_along(block, axis, distance):
    devices = range(lax.axis_size(axis))
    route = [((i - distance) % len(devices), i) for i in devices]
    return lax.ppermute(block, axis, route)


def fold_rows(running, left_side, portion):
    return running + jnp.dot(left_side, portion, preferred_element_type=jnp.float32)


def ring_shards(
    queries,
    keys_values,
    surface,
    out_weight,
    up_weight,
    down_weight,
    norm_gain,
    block_lists,
    list_lengths,
):
    row_count, feature_width = queries.shape
    query_blocks = block_lists.shape[0]
    block_rows = row_count // query_blocks
    loop_size = lax.axis_size(("blk", "head"))
    cycle_reach = min(3, (loop_size - 1) // 2)
    own_index = lax.axis_index(("blk", "head"))
    query_heads = queries.reshape(query_blocks, block_rows, HEADS, HD)
    score_scale = 1.0 / HD**0.5
    entry_live = jnp.arange(LIST, dtype=jnp.int32)[None, :] < list_lengths[:, None]
    start_state = (
        jnp.full((query_blocks, HEADS, block_rows), -1e30, jnp.float32),
        jnp.zeros((query_blocks, HEADS, block_rows), jnp.float32),
        jnp.zeros((query_blocks, HEADS, block_rows, HD), jnp.float32),
    )

    def absorb(softmax_state, anchor_pair, source):
        listed = jnp.any((block_lists == source) & entry_live, axis=1)
        running_max, running_sum, running_acc = softmax_state
        block_keys = anchor_pair[0].reshape(block_rows, HEADS, HD)
        block_values = anchor_pair[1].reshape(block_rows, HEADS, HD)
        scores = (
            jnp.einsum(
                "bqhd,khd->bhqk", query_heads, block_keys, preferred_element_type=jnp.float32
            )
            * score_scale
        )
        block_max = jnp.max(scores, axis=3)
        new_max = jnp.where(listed[:, None, None], jnp.maximum(running_max, block_max), running_max)
        ratio = jnp.exp(running_max - new_max)
        weights_exp = jnp.where(
            listed[:, None, None, None], jnp.exp(scores - new_max[..., None]), 0.0
        )
        new_sum = running_sum * ratio + jnp.sum(weights_exp, axis=3)
        probs = weights_exp.astype(jnp.bfloat16)
        new_acc = running_acc * ratio[..., None] + jnp.einsum(
            "bhqk,khd->bhqd", probs, block_values, preferred_element_type=jnp.float32
        )
        return (new_max, new_sum, new_acc)

    moving = passed_along(keys_values, ("blk", "head"), -cycle_reach)
    source = (own_index + cycle_reach) % loop_size
    softmax_state = absorb(start_state, moving, source)
    for cycle_turn in range(2 * cycle_reach):
        moving = passed_along(moving, ("blk", "head"), 1)
        source = (source - 1) % loop_size
        softmax_state = absorb(softmax_state, moving, source)
    final_max, final_sum, final_acc = softmax_state
    context = final_acc / final_sum[..., None]
    context = (
        jnp.transpose(context, (0, 2, 1, 3)).reshape(row_count, feature_width).astype(jnp.bfloat16)
    )
    residual = surface.astype(jnp.float32)
    hidden = fold_rows(residual, context, lax.all_gather(out_weight, "head", axis=0, tiled=True))
    mean_square = jnp.mean(hidden * hidden, axis=1, keepdims=True)
    normed = (hidden * lax.rsqrt(mean_square + 1e-05) * norm_gain[None, :]).astype(jnp.bfloat16)
    up_start = jnp.zeros((row_count, up_weight.shape[1]), jnp.float32)
    pre_gelu = fold_rows(up_start, normed, lax.all_gather(up_weight, "head", axis=0, tiled=True))
    activated = jax.nn.gelu(pre_gelu, approximate=True).astype(jnp.bfloat16)
    mixed_out = fold_rows(
        hidden, activated, lax.all_gather(down_weight, "head", axis=0, tiled=True)
    )
    return mixed_out.astype(jnp.bfloat16)


AXES = ("blk", "head", "side", "core")
SIZES = (2, 4, 2, 2)
DEVICES = list(itertools.product(*(range(size) for size in SIZES)))
ZS = 4
HZ = HEADS // ZS
NOTE = 16
ANY = pl.BlockSpec(memory_space=pl.ANY)
SMEM = pl.BlockSpec(memory_space=pltpu.SMEM)
VMEM = pl.BlockSpec(memory_space=pltpu.VMEM)
HBM = pl.BlockSpec(memory_space=pltpu.HBM)


def flat(x, z, y, c):
    return ((x * SIZES[1] + z) * SIZES[2] + y) * SIZES[3] + c


def sent(value, route):
    return lax.ppermute(value, AXES, [(flat(*d), flat(*route(*d))) for d in DEVICES])


def across_head(slot):
    return lambda x, z, y, c: (x, z ^ slot, y, c)


def over_blk(x, z, y, c):
    return (1 - x, z, y, c)


def plane_first(x, z, y, c):
    return (1 - x, z, y, c) if c == 0 else (x, z, 1 - y, c)


def plane_second(x, z, y, c):
    return (x, z, 1 - y, c) if c == 0 else (1 - x, z, y, c)


def other_core(x, z, y, c):
    return (x, z, y, 1 - c)


def after(value, *earlier):
    return lax.optimization_barrier((value,) + earlier)[0]


def pack_kernel(listed_hbm, length_hbm, q_hbm, kv_hbm, out_w, up_w, down_w, *refs):
    kv_slots, q_slots, piece = refs[:ZS], refs[ZS : 2 * ZS], refs[2 * ZS]
    kv_all, q_all, q_ref, kv_ref, listed, length, sems = refs[2 * ZS + 1 :]
    x, z, y, c = (lax.axis_index(axis) for axis in AXES)
    p = 2 * x + y
    m = 2 * p + c
    ro, cols = out_w.shape[0] // 4, out_w.shape[1] // 2
    ru, rd = up_w.shape[0], down_w.shape[0] // 8
    rows = [ro, ro + ru, ro + ru + rd]
    copies = [
        pltpu.make_async_copy(kv_hbm, kv_ref, sems.at[0]),
        pltpu.make_async_copy(q_hbm, q_ref, sems.at[1]),
        pltpu.make_async_copy(listed_hbm, listed, sems.at[3]),
        pltpu.make_async_copy(length_hbm, length, sems.at[4]),
    ]
    copies += [
        pltpu.make_async_copy(
            out_w.at[pl.ds(pl.multiple_of(p * ro, 16), ro), pl.ds(pl.multiple_of(c * cols, 128), cols)],
            piece.at[0, pl.ds(0, ro)],
            sems.at[2],
        ),
        pltpu.make_async_copy(
            up_w.at[:, pl.ds(pl.multiple_of(m * cols, 128), cols)],
            piece.at[0, pl.ds(rows[0], ru)],
            sems.at[2],
        ),
    ]
    for side in range(2):
        copies.append(
            pltpu.make_async_copy(
                down_w.at[pl.ds(pl.multiple_of(m * rd, 16), rd), pl.ds(side * cols, cols)],
                piece.at[0, pl.ds(rows[1 + side], rd)],
                sems.at[2],
            )
        )
    for copy in copies:
        copy.start()
    n = q_ref.shape[0] // 2
    copies[0].wait()
    for pair in range(HEADS // 2):
        lanes = slice(pair * 2 * HD, (pair + 1) * 2 * HD)
        keys, values = kv_ref[0, :, lanes], kv_ref[1, :, lanes]
        even, odd = 2 * pair, 2 * pair + 1
        low = lax.broadcasted_iota(jnp.int32, keys.shape, 1) < HD
        kv_all[even // HZ, even % HZ] = jnp.where(low, keys, pltpu.roll(values, HD, 1))
        kv_all[odd // HZ, odd % HZ] = jnp.where(low, pltpu.roll(keys, HD, 1), values)
    copies[1].wait()
    for pair in range(HEADS // 2):
        lanes = slice(pair * 2 * HD, (pair + 1) * 2 * HD)
        upper, lower = q_ref[:n, lanes], q_ref[n:, lanes]
        even, odd = 2 * pair, 2 * pair + 1
        low = lax.broadcasted_iota(jnp.int32, upper.shape, 1) < HD
        q_all[even // HZ, (even % HZ) * n : (even % HZ + 1) * n] = jnp.where(
            low, upper, pltpu.roll(lower, HD, 1)
        )
        q_all[odd // HZ, (odd % HZ) * n : (odd % HZ + 1) * n] = jnp.where(
            low, pltpu.roll(upper, HD, 1), lower
        )
    copies[2].wait()
    copies[3].wait()
    lane = lax.broadcasted_iota(jnp.int32, (NOTE, 2 * HD), 1)
    note = jnp.where(lane == LIST, length[0], 0)
    for j in range(LIST):
        note = jnp.where(lane == j, listed[0, j], note)
    note = note.astype(jnp.float32).astype(jnp.bfloat16)
    for s in range(ZS):
        there = jnp.bitwise_xor(z, s)
        kv_slots[s][...] = kv_all[there]
        q_slots[s][: HZ * n] = q_all[there]
        q_slots[s][HZ * n :] = note
    for copy in copies[4:]:
        copy.wait()


def packed(listed, length, queries, keys_values, out_weight, up_weight, down_weight):
    rows, width = queries.shape
    cols = width // 2
    piece_rows = out_weight.shape[0] // 4 + up_weight.shape[0] + down_weight.shape[0] // 4
    kv_shape, q_rows = (HZ, rows, 2 * HD), HZ * rows // 2
    made = lambda shape: jax.ShapeDtypeStruct(shape, jnp.bfloat16)
    outs = pl.pallas_call(
        pack_kernel,
        out_shape=[made(kv_shape)] * ZS + [made((q_rows + NOTE, 2 * HD))] * ZS + [made((1, piece_rows, cols))],
        in_specs=[HBM] * 7,
        out_specs=[VMEM] * (2 * ZS + 1),
        scratch_shapes=[
            pltpu.VMEM((ZS,) + kv_shape, jnp.bfloat16),
            pltpu.VMEM((ZS, q_rows, 2 * HD), jnp.bfloat16),
            pltpu.VMEM(queries.shape, jnp.bfloat16),
            pltpu.VMEM(keys_values.shape, jnp.bfloat16),
            pltpu.SMEM(listed.shape, jnp.int32),
            pltpu.SMEM(length.shape, jnp.int32),
            pltpu.SemaphoreType.DMA((5,)),
        ],
        compiler_params=pltpu.CompilerParams(vmem_limit_bytes=55 * MIB),
        cost_estimate=pl.CostEstimate(flops=0, bytes_accessed=4 * MIB, transcendentals=0),
        name="pack_heads",
    )(listed, length, queries, keys_values, out_weight, up_weight, down_weight)
    return outs[:ZS], outs[ZS : 2 * ZS], outs[2 * ZS]


def attend_kernel(blocks, *refs):
    q_refs, o_refs = refs[: len(refs) // 2], refs[len(refs) // 2 :]
    x, z = (lax.axis_index(axis) for axis in AXES[:2])
    n = o_refs[0].shape[1]
    low = lax.broadcasted_iota(jnp.int32, (n, 2 * HD), 1) < HD
    key_lanes = lax.broadcasted_iota(jnp.int32, (2 * n, 2 * HD), 1) < HD
    scale = LOG2E / HD**0.5
    row = lax.broadcasted_iota(jnp.int32, (NOTE, 2 * HD), 0)
    lane = lax.broadcasted_iota(jnp.int32, (NOTE, 2 * HD), 1)
    digit = jnp.left_shift(1, 3 * jnp.minimum(lane, LIST))
    digit = jnp.where((row == 0) & (lane <= LIST), digit, 0).astype(jnp.float32)
    codes = [
        jnp.sum(q_ref[HZ * n :].astype(jnp.float32) * digit).astype(jnp.int32) for q_ref in q_refs
    ]
    for q_ref, o_ref, code in zip(q_refs, o_refs, codes):
        at = []
        for j in range(LIST):
            block = jnp.bitwise_and(jnp.right_shift(code, 3 * j), 7)
            side, source = block // ZS, lax.rem(block, ZS)
            at.append(jnp.where(side == x, 0, ZS) + jnp.bitwise_xor(z, source))
        length = jnp.right_shift(code, 3 * LIST)

        def scored(h, count, q_ref=q_ref, at=at):
            pair = q_ref[h * n : (h + 1) * n]
            none = jnp.zeros_like(pair)
            q = jnp.concatenate(
                [jnp.where(low, pair, none), jnp.where(low, pltpu.roll(pair, HD, 1), none)], axis=0
            )
            scores = [
                lax.dot_general(
                    q, blocks[at[j], h], (((1,), (1,)), ((), ())), preferred_element_type=jnp.float32
                )
                for j in range(count)
            ]
            return scores, jnp.max(functools.reduce(jnp.maximum, scores), axis=1, keepdims=True)

        def summed(h, count, scores, top, o_ref=o_ref, at=at):
            acc = None
            for j in range(count):
                weights = jnp.exp2((scores[j] - top) * scale).astype(jnp.bfloat16)
                values = blocks[at[j], h]
                values = jnp.where(key_lanes, jnp.ones_like(values), values)
                part = jnp.dot(weights, values, preferred_element_type=jnp.float32)
                acc = part if j == 0 else acc + part
            result = acc / pltpu.roll(acc, HD, 1)
            upper, lower = result[:n], result[n:]
            o_ref[h] = jnp.where(low, pltpu.roll(upper, HD, 1), lower).astype(jnp.bfloat16)

        for count in range(1, LIST + 1):

            @pl.when(length == count)
            def _(count=count, scored=scored, summed=summed):
                held = [scored(h, count) for h in range(HZ)]
                for h in range(HZ):
                    summed(h, count, *held[h])


def attended(blocks, queries):
    made = jax.ShapeDtypeStruct((HZ, blocks.shape[2] // 2, 2 * HD), jnp.bfloat16)
    return pl.pallas_call(
        attend_kernel,
        out_shape=[made] * len(queries),
        in_specs=[VMEM] * (1 + len(queries)),
        out_specs=[VMEM] * len(queries),
        compiler_params=pltpu.CompilerParams(vmem_limit_bytes=16 * MIB),
        cost_estimate=pl.CostEstimate(
            flops=5 * 10**8, bytes_accessed=MIB, transcendentals=8 * 10**5
        ),
        name="attend",
    )(blocks, *queries)


def laid(copies, ref, swapped, later, shapes, into, sems):
    x, z, y, c = (lax.axis_index(axis) for axis in AXES)
    out_all, up_all, down_all = into
    (rs, width), ru, rd = shapes
    cols, ro = width // 2, rs // 4
    rows = [ro, ro + ru, ro + ru + rd]
    core = 1 - c if swapped else c
    first_x, first_y = jnp.where(core == 0, 1 - x, x), jnp.where(core == 0, y, 1 - y)
    second_x, second_y = jnp.where(core == 0, x, 1 - x), jnp.where(core == 0, 1 - y, y)
    mine, far = (x, y), (1 - x, 1 - y)
    first, second = (first_x, first_y), (second_x, second_y)
    if later:
        pieces = [(2, second), (3, second), (3, far)]
    else:
        pieces = [(k, who) for who in (mine, first, far) for k in (1, 2)]
        pieces += [(1, second), (3, mine), (3, first)]
    for at, (k, (px, py)) in enumerate(pieces):
        source = jnp.bitwise_xor(z, k)
        slot_row = k * rs
        p = 2 * px + py
        m = 2 * p + core
        piece = ref.at[at]
        copies.append(
            pltpu.make_async_copy(
                piece.at[pl.ds(0, ro)],
                out_all.at[
                    pl.ds(pl.multiple_of(slot_row + p * ro, 16), ro),
                    pl.ds(pl.multiple_of(core * cols, 128), cols),
                ],
                sems.at[0],
            )
        )
        copies.append(
            pltpu.make_async_copy(
                piece.at[pl.ds(rows[0], ru)],
                up_all.at[
                    pl.ds(pl.multiple_of(source * ru, 16), ru),
                    pl.ds(pl.multiple_of(m * cols, 128), cols),
                ],
                sems.at[1],
            )
        )
        for side in range(2):
            copies.append(
                pltpu.make_async_copy(
                    piece.at[pl.ds(rows[1 + side], rd)],
                    down_all.at[
                        pl.ds(pl.multiple_of((source * 8 + m) * rd, 16), rd),
                        pl.ds(side * cols, cols),
                    ],
                    sems.at[2],
                )
            )


def gather_kernel(out_w, up_w, down_w, early, early_swapped, late, *refs):
    out_all, up_all, down_all, sems = refs
    z = lax.axis_index("head")
    rs, ru, rd = out_w.shape[0], up_w.shape[0], down_w.shape[0]
    copies = [
        pltpu.make_async_copy(out_w, out_all.at[pl.ds(0, rs)], sems.at[0]),
        pltpu.make_async_copy(
            up_w, up_all.at[pl.ds(pl.multiple_of(z * ru, 16), ru)], sems.at[1]
        ),
        pltpu.make_async_copy(
            down_w, down_all.at[pl.ds(pl.multiple_of(z * rd, 16), rd)], sems.at[2]
        ),
    ]
    shapes = (out_w.shape, ru, rd // 8)
    laid(copies, early, False, False, shapes, refs[:3], sems)
    laid(copies, early_swapped, True, False, shapes, refs[:3], sems)
    laid(copies, late, False, True, shapes, refs[:3], sems)
    for copy in copies:
        copy.start()
    for copy in copies:
        copy.wait()


def gathered(out_weight, up_weight, down_weight, *held):
    width, hidden_units = up_weight.shape[0] * ZS, up_weight.shape[1]
    made = lambda *shape: jax.ShapeDtypeStruct(shape, jnp.bfloat16)
    return pl.pallas_call(
        gather_kernel,
        out_shape=[made(width, width), made(width, hidden_units), made(hidden_units, width)],
        in_specs=[ANY] * (3 + len(held)),
        out_specs=[VMEM] * 3,
        scratch_shapes=[pltpu.SemaphoreType.DMA((3,))],
        compiler_params=pltpu.CompilerParams(vmem_limit_bytes=20 * MIB),
        cost_estimate=pl.CostEstimate(flops=0, bytes_accessed=12 * MIB, transcendentals=0),
        name="gather",
    )(out_weight, up_weight, down_weight, *held)


def feed_kernel(gain, surface, *refs):
    ctx_slots, refs = refs[:ZS], refs[ZS + 3 :]
    late_swapped, o_ref, out_all, up_all, down_all, sems = refs
    width, hidden_units = up_all.shape
    copies = []
    shapes = ((width // ZS, width), width // ZS, hidden_units // ZS // 8)
    laid(copies, late_swapped, True, True, shapes, (out_all, up_all, down_all), sems)
    first = [copies[i] for i in range(len(copies)) if i % 4 == 0]
    second = [copies[i] for i in range(len(copies)) if i % 4 == 1]
    third = [copies[i] for i in range(len(copies)) if i % 4 > 1]
    for copy in first + second + third:
        copy.start()

    tiles = [ctx_slots[s][h] for s in range(ZS) for h in range(HZ)]
    low = lax.broadcasted_iota(jnp.int32, tiles[0].shape, 1) < HD
    upper, lower = [], []
    for left, right in zip(tiles[::2], tiles[1::2]):
        upper.append(jnp.where(low, left, pltpu.roll(right, HD, 1)))
        lower.append(jnp.where(low, pltpu.roll(left, HD, 1), right))
    context = jnp.concatenate(
        [jnp.concatenate(upper, axis=1), jnp.concatenate(lower, axis=1)], axis=0
    )
    for copy in first:
        copy.wait()
    hidden = surface[...].astype(jnp.float32) + jnp.dot(
        context, out_all[...], preferred_element_type=jnp.float32
    )
    mean_square = jnp.mean(hidden * hidden, axis=1, keepdims=True)
    normed = (hidden * lax.rsqrt(mean_square + 1e-05) * gain[...]).astype(jnp.bfloat16)
    for copy in second:
        copy.wait()
    total = hidden
    for step in range(hidden_units // width):
        pre = jnp.dot(
            normed, up_all[:, step * width : (step + 1) * width], preferred_element_type=jnp.float32
        )
        act = jax.nn.gelu(pre, approximate=True).astype(jnp.bfloat16)
        if step == 0:
            for copy in third:
                copy.wait()
        total = total + jnp.dot(
            act, down_all[step * width : (step + 1) * width, :], preferred_element_type=jnp.float32
        )
    o_ref[...] = total.astype(jnp.bfloat16)


def fed(gain, surface, ctx_slots, weights, late_swapped):
    outs = pl.pallas_call(
        feed_kernel,
        out_shape=[jax.ShapeDtypeStruct(v.shape, jnp.bfloat16) for v in (surface, *weights)],
        in_specs=[VMEM, VMEM] + [VMEM] * (ZS + 3) + [ANY],
        out_specs=[VMEM] * 4,
        scratch_shapes=[pltpu.SemaphoreType.DMA((3,))],
        input_output_aliases={2 + ZS: 1, 3 + ZS: 2, 4 + ZS: 3},
        compiler_params=pltpu.CompilerParams(vmem_limit_bytes=30 * MIB),
        cost_estimate=pl.CostEstimate(
            flops=3 * 10**9, bytes_accessed=12 * MIB, transcendentals=10**6
        ),
        name="feed",
    )(gain, surface, *ctx_slots, *weights, late_swapped)
    return outs[0]


def split_shards(
    queries,
    keys_values,
    surface,
    out_weight,
    up_weight,
    down_weight,
    norm_gain,
    block_lists,
    list_lengths,
):
    kv_slots, q_slots, piece = packed(
        block_lists, list_lengths, queries, keys_values, out_weight, up_weight, down_weight
    )
    kv_slots, q_slots = list(kv_slots), list(q_slots)
    near, q, far = {0: kv_slots[0]}, {0: q_slots[0]}, {}
    w12 = jnp.concatenate([sent(piece, across_head(k)) for k in (1, 2)])
    far[0] = sent(kv_slots[0], over_blk)
    near[1], near[3] = (sent(kv_slots[s], across_head(s)) for s in (1, 3))
    w12, near[1], near[3], far[0], kv_slots[2] = lax.optimization_barrier(
        (w12, near[1], near[3], far[0], kv_slots[2])
    )
    first12 = sent(w12, plane_first)
    far13 = sent(jnp.stack([near[1], near[3]]), over_blk)
    near[2] = sent(kv_slots[2], across_head(2))
    w3 = sent(w12[1:], across_head(1))
    near[2], w3, q_slots[1], q_slots[2], q_slots[3] = lax.optimization_barrier(
        (near[2], w3, q_slots[1], q_slots[2], q_slots[3])
    )
    far[2] = sent(near[2], over_blk)
    more12 = sent(jnp.concatenate([first12, w12[:1]]), plane_second)
    first12, far13, near[2], w3 = lax.optimization_barrier((first12, far13, near[2], w3))
    far[1], far[3] = far13[0], far13[1]
    away = (2, 1, 3)
    for s in away:
        q[s] = sent(q_slots[s], across_head(s))
    more3 = sent(first12[1:], across_head(1))
    blocks = jnp.stack([near[s] for s in range(ZS)] + [far[s] for s in range(ZS)])
    ctx_slots = dict(zip(away, attended(blocks, [q[s] for s in away])))
    more12, more3 = after(more12, ctx_slots[2]), after(more3, ctx_slots[2])
    early = jnp.concatenate([w12, first12, more12, w3, more3])
    late = sent(jnp.concatenate([w12[1:], w3, more3]), plane_second)
    for s in away:
        ctx_slots[s] = sent(ctx_slots[s], across_head(s))
    (ctx_slots[0],) = attended(blocks, [q[0]])
    early_swapped = sent(after(early, ctx_slots[0]), other_core)
    late = after(late, ctx_slots[0], ctx_slots[1], ctx_slots[2], ctx_slots[3])
    late_swapped = sent(late, other_core)
    whole = gathered(out_weight, up_weight, down_weight, early, early_swapped, late)
    ctx_slots = [ctx_slots[s] for s in range(ZS)]
    return fed(norm_gain[None, :], surface, ctx_slots, whole, late_swapped)


def solution(mesh):
    sizes = (mesh.shape["blk"], mesh.shape["head"], mesh.shape["bend"])
    if sizes == (2, 4, 4):
        mesh = Mesh(mesh.devices.reshape(SIZES), AXES)
        parts, shards = ("side", "core"), split_shards
    else:
        parts, shards = ("bend",), ring_shards
    rows = parts + ("blk", "head")
    return jax.shard_map(
        shards,
        mesh=mesh,
        in_specs=(
            P(rows, None),
            P(None, rows, None),
            P(rows, None),
            P("head", None),
            P("head", None),
            P("head", None),
            P(),
            P(rows, None),
            P(rows),
        ),
        out_specs=P(rows, None),
        check_vma=False,
    )
```

```python
import functools
import itertools

import jax
import jax.numpy as jnp
from jax import lax
from jax.experimental import pallas as pl
from jax.experimental.pallas import tpu as pltpu
from jax.sharding import Mesh
from jax.sharding import PartitionSpec as P

HEADS = 12
HD = 64
LIST = 4
MIB = 1024 * 1024
LOG2E = 1.4426950408889634


def passed_along(block, axis, distance):
    devices = range(lax.axis_size(axis))
    route = [((i - distance) % len(devices), i) for i in devices]
    return lax.ppermute(block, axis, route)


def fold_rows(running, left_side, portion):
    return running + jnp.dot(left_side, portion, preferred_element_type=jnp.float32)


def ring_shards(
    queries,
    keys_values,
    surface,
    out_weight,
    up_weight,
    down_weight,
    norm_gain,
    block_lists,
    list_lengths,
):
    row_count, feature_width = queries.shape
    query_blocks = block_lists.shape[0]
    block_rows = row_count // query_blocks
    loop_size = lax.axis_size(("blk", "head"))
    cycle_reach = min(3, (loop_size - 1) // 2)
    own_index = lax.axis_index(("blk", "head"))
    query_heads = queries.reshape(query_blocks, block_rows, HEADS, HD)
    score_scale = 1.0 / HD**0.5
    entry_live = jnp.arange(LIST, dtype=jnp.int32)[None, :] < list_lengths[:, None]
    start_state = (
        jnp.full((query_blocks, HEADS, block_rows), -1e30, jnp.float32),
        jnp.zeros((query_blocks, HEADS, block_rows), jnp.float32),
        jnp.zeros((query_blocks, HEADS, block_rows, HD), jnp.float32),
    )

    def absorb(softmax_state, anchor_pair, source):
        listed = jnp.any((block_lists == source) & entry_live, axis=1)
        running_max, running_sum, running_acc = softmax_state
        block_keys = anchor_pair[0].reshape(block_rows, HEADS, HD)
        block_values = anchor_pair[1].reshape(block_rows, HEADS, HD)
        scores = (
            jnp.einsum(
                "bqhd,khd->bhqk", query_heads, block_keys, preferred_element_type=jnp.float32
            )
            * score_scale
        )
        block_max = jnp.max(scores, axis=3)
        new_max = jnp.where(listed[:, None, None], jnp.maximum(running_max, block_max), running_max)
        ratio = jnp.exp(running_max - new_max)
        weights_exp = jnp.where(
            listed[:, None, None, None], jnp.exp(scores - new_max[..., None]), 0.0
        )
        new_sum = running_sum * ratio + jnp.sum(weights_exp, axis=3)
        probs = weights_exp.astype(jnp.bfloat16)
        new_acc = running_acc * ratio[..., None] + jnp.einsum(
            "bhqk,khd->bhqd", probs, block_values, preferred_element_type=jnp.float32
        )
        return (new_max, new_sum, new_acc)

    moving = passed_along(keys_values, ("blk", "head"), -cycle_reach)
    source = (own_index + cycle_reach) % loop_size
    softmax_state = absorb(start_state, moving, source)
    for cycle_turn in range(2 * cycle_reach):
        moving = passed_along(moving, ("blk", "head"), 1)
        source = (source - 1) % loop_size
        softmax_state = absorb(softmax_state, moving, source)
    final_max, final_sum, final_acc = softmax_state
    context = final_acc / final_sum[..., None]
    context = (
        jnp.transpose(context, (0, 2, 1, 3)).reshape(row_count, feature_width).astype(jnp.bfloat16)
    )
    residual = surface.astype(jnp.float32)
    hidden = fold_rows(residual, context, lax.all_gather(out_weight, "head", axis=0, tiled=True))
    mean_square = jnp.mean(hidden * hidden, axis=1, keepdims=True)
    normed = (hidden * lax.rsqrt(mean_square + 1e-05) * norm_gain[None, :]).astype(jnp.bfloat16)
    up_start = jnp.zeros((row_count, up_weight.shape[1]), jnp.float32)
    pre_gelu = fold_rows(up_start, normed, lax.all_gather(up_weight, "head", axis=0, tiled=True))
    activated = jax.nn.gelu(pre_gelu, approximate=True).astype(jnp.bfloat16)
    mixed_out = fold_rows(
        hidden, activated, lax.all_gather(down_weight, "head", axis=0, tiled=True)
    )
    return mixed_out.astype(jnp.bfloat16)


AXES = ("blk", "head", "side", "core")
SIZES = (2, 4, 2, 2)
DEVICES = list(itertools.product(*(range(size) for size in SIZES)))
ZS = 4
HZ = HEADS // ZS
NOTE = 16
ANY = pl.BlockSpec(memory_space=pl.ANY)
SMEM = pl.BlockSpec(memory_space=pltpu.SMEM)
VMEM = pl.BlockSpec(memory_space=pltpu.VMEM)
HBM = pl.BlockSpec(memory_space=pltpu.HBM)


def flat(x, z, y, c):
    return ((x * SIZES[1] + z) * SIZES[2] + y) * SIZES[3] + c


def sent(value, route):
    return lax.ppermute(value, AXES, [(flat(*d), flat(*route(*d))) for d in DEVICES])


def across_head(slot):
    return lambda x, z, y, c: (x, z ^ slot, y, c)


def over_blk(x, z, y, c):
    return (1 - x, z, y, c)


def plane_first(x, z, y, c):
    return (1 - x, z, y, c) if c == 0 else (x, z, 1 - y, c)


def plane_second(x, z, y, c):
    return (x, z, 1 - y, c) if c == 0 else (1 - x, z, y, c)


def other_core(x, z, y, c):
    return (x, z, y, 1 - c)


def after(value, *earlier):
    return lax.optimization_barrier((value,) + earlier)[0]


def pack_kernel(listed_hbm, length_hbm, q_hbm, kv_hbm, out_w, up_w, down_w, *refs):
    kv_slots, q_slots, piece = refs[:ZS], refs[ZS : 2 * ZS], refs[2 * ZS]
    kv_all, q_all, q_ref, kv_ref, listed, length, sems = refs[2 * ZS + 1 :]
    x, z, y, c = (lax.axis_index(axis) for axis in AXES)
    p = 2 * x + y
    m = 2 * p + c
    ro, cols = out_w.shape[0] // 4, out_w.shape[1] // 2
    ru, rd = up_w.shape[0], down_w.shape[0] // 8
    rows = [ro, ro + ru, ro + ru + rd]
    copies = [
        pltpu.make_async_copy(kv_hbm, kv_ref, sems.at[0]),
        pltpu.make_async_copy(q_hbm, q_ref, sems.at[1]),
        pltpu.make_async_copy(listed_hbm, listed, sems.at[3]),
        pltpu.make_async_copy(length_hbm, length, sems.at[4]),
    ]
    copies += [
        pltpu.make_async_copy(
            out_w.at[pl.ds(pl.multiple_of(p * ro, 16), ro), pl.ds(pl.multiple_of(c * cols, 128), cols)],
            piece.at[0, pl.ds(0, ro)],
            sems.at[2],
        ),
        pltpu.make_async_copy(
            up_w.at[:, pl.ds(pl.multiple_of(m * cols, 128), cols)],
            piece.at[0, pl.ds(rows[0], ru)],
            sems.at[2],
        ),
    ]
    for side in range(2):
        copies.append(
            pltpu.make_async_copy(
                down_w.at[pl.ds(pl.multiple_of(m * rd, 16), rd), pl.ds(side * cols, cols)],
                piece.at[0, pl.ds(rows[1 + side], rd)],
                sems.at[2],
            )
        )
    for copy in copies:
        copy.start()
    n = q_ref.shape[0] // 2
    copies[0].wait()
    for pair in range(HEADS // 2):
        lanes = slice(pair * 2 * HD, (pair + 1) * 2 * HD)
        keys, values = kv_ref[0, :, lanes], kv_ref[1, :, lanes]
        even, odd = 2 * pair, 2 * pair + 1
        low = lax.broadcasted_iota(jnp.int32, keys.shape, 1) < HD
        kv_all[even // HZ, even % HZ] = jnp.where(low, keys, pltpu.roll(values, HD, 1))
        kv_all[odd // HZ, odd % HZ] = jnp.where(low, pltpu.roll(keys, HD, 1), values)
    copies[1].wait()
    for pair in range(HEADS // 2):
        lanes = slice(pair * 2 * HD, (pair + 1) * 2 * HD)
        upper, lower = q_ref[:n, lanes], q_ref[n:, lanes]
        even, odd = 2 * pair, 2 * pair + 1
        low = lax.broadcasted_iota(jnp.int32, upper.shape, 1) < HD
        q_all[even // HZ, (even % HZ) * n : (even % HZ + 1) * n] = jnp.where(
            low, upper, pltpu.roll(lower, HD, 1)
        )
        q_all[odd // HZ, (odd % HZ) * n : (odd % HZ + 1) * n] = jnp.where(
            low, pltpu.roll(upper, HD, 1), lower
        )
    copies[2].wait()
    copies[3].wait()
    lane = lax.broadcasted_iota(jnp.int32, (NOTE, 2 * HD), 1)
    note = jnp.where(lane == LIST, length[0], 0)
    for j in range(LIST):
        note = jnp.where(lane == j, listed[0, j], note)
    note = note.astype(jnp.float32).astype(jnp.bfloat16)
    for s in range(ZS):
        there = jnp.bitwise_xor(z, s)
        kv_slots[s][...] = kv_all[there]
        q_slots[s][: HZ * n] = q_all[there]
        q_slots[s][HZ * n :] = note
    for copy in copies[4:]:
        copy.wait()


def packed(listed, length, queries, keys_values, out_weight, up_weight, down_weight):
    rows, width = queries.shape
    cols = width // 2
    piece_rows = out_weight.shape[0] // 4 + up_weight.shape[0] + down_weight.shape[0] // 4
    kv_shape, q_rows = (HZ, rows, 2 * HD), HZ * rows // 2
    made = lambda shape: jax.ShapeDtypeStruct(shape, jnp.bfloat16)
    outs = pl.pallas_call(
        pack_kernel,
        out_shape=[made(kv_shape)] * ZS + [made((q_rows + NOTE, 2 * HD))] * ZS + [made((1, piece_rows, cols))],
        in_specs=[HBM] * 7,
        out_specs=[VMEM] * (2 * ZS + 1),
        scratch_shapes=[
            pltpu.VMEM((ZS,) + kv_shape, jnp.bfloat16),
            pltpu.VMEM((ZS, q_rows, 2 * HD), jnp.bfloat16),
            pltpu.VMEM(queries.shape, jnp.bfloat16),
            pltpu.VMEM(keys_values.shape, jnp.bfloat16),
            pltpu.SMEM(listed.shape, jnp.int32),
            pltpu.SMEM(length.shape, jnp.int32),
            pltpu.SemaphoreType.DMA((5,)),
        ],
        compiler_params=pltpu.CompilerParams(vmem_limit_bytes=55 * MIB),
        cost_estimate=pl.CostEstimate(flops=0, bytes_accessed=4 * MIB, transcendentals=0),
        name="pack_heads",
    )(listed, length, queries, keys_values, out_weight, up_weight, down_weight)
    return outs[:ZS], outs[ZS : 2 * ZS], outs[2 * ZS]


def attend_kernel(blocks, *refs):
    q_refs, o_refs = refs[: len(refs) // 2], refs[len(refs) // 2 :]
    x, z = (lax.axis_index(axis) for axis in AXES[:2])
    n = o_refs[0].shape[1]
    low = lax.broadcasted_iota(jnp.int32, (n, 2 * HD), 1) < HD
    key_lanes = lax.broadcasted_iota(jnp.int32, (2 * n, 2 * HD), 1) < HD
    scale = LOG2E / HD**0.5
    row = lax.broadcasted_iota(jnp.int32, (NOTE, 2 * HD), 0)
    lane = lax.broadcasted_iota(jnp.int32, (NOTE, 2 * HD), 1)
    digit = jnp.left_shift(1, 3 * jnp.minimum(lane, LIST))
    digit = jnp.where((row == 0) & (lane <= LIST), digit, 0).astype(jnp.float32)
    codes = [
        jnp.sum(q_ref[HZ * n :].astype(jnp.float32) * digit).astype(jnp.int32) for q_ref in q_refs
    ]
    for q_ref, o_ref, code in zip(q_refs, o_refs, codes):
        at = []
        for j in range(LIST):
            block = jnp.bitwise_and(jnp.right_shift(code, 3 * j), 7)
            side, source = block // ZS, lax.rem(block, ZS)
            at.append(jnp.where(side == x, 0, ZS) + jnp.bitwise_xor(z, source))
        length = jnp.right_shift(code, 3 * LIST)

        def scored(h, count, q_ref=q_ref, at=at):
            pair = q_ref[h * n : (h + 1) * n]
            none = jnp.zeros_like(pair)
            q = jnp.concatenate(
                [jnp.where(low, pair, none), jnp.where(low, pltpu.roll(pair, HD, 1), none)], axis=0
            )
            scores = [
                lax.dot_general(
                    q, blocks[at[j], h], (((1,), (1,)), ((), ())), preferred_element_type=jnp.float32
                )
                for j in range(count)
            ]
            return scores, jnp.max(functools.reduce(jnp.maximum, scores), axis=1, keepdims=True)

        def summed(h, count, scores, top, o_ref=o_ref, at=at):
            acc = None
            for j in range(count):
                weights = jnp.exp2((scores[j] - top) * scale).astype(jnp.bfloat16)
                values = blocks[at[j], h]
                values = jnp.where(key_lanes, jnp.ones_like(values), values)
                part = jnp.dot(weights, values, preferred_element_type=jnp.float32)
                acc = part if j == 0 else acc + part
            result = acc / pltpu.roll(acc, HD, 1)
            upper, lower = result[:n], result[n:]
            o_ref[h] = jnp.where(low, pltpu.roll(upper, HD, 1), lower).astype(jnp.bfloat16)

        for count in range(1, LIST + 1):

            @pl.when(length == count)
            def _(count=count, scored=scored, summed=summed):
                held = [scored(h, count) for h in range(HZ)]
                for h in range(HZ):
                    summed(h, count, *held[h])


def attended(blocks, queries):
    made = jax.ShapeDtypeStruct((HZ, blocks.shape[2] // 2, 2 * HD), jnp.bfloat16)
    return pl.pallas_call(
        attend_kernel,
        out_shape=[made] * len(queries),
        in_specs=[VMEM] * (1 + len(queries)),
        out_specs=[VMEM] * len(queries),
        compiler_params=pltpu.CompilerParams(vmem_limit_bytes=16 * MIB),
        cost_estimate=pl.CostEstimate(
            flops=5 * 10**8, bytes_accessed=MIB, transcendentals=8 * 10**5
        ),
        name="attend",
    )(blocks, *queries)


def laid(copies, ref, swapped, later, shapes, into, sems):
    x, z, y, c = (lax.axis_index(axis) for axis in AXES)
    out_all, up_all, down_all = into
    (rs, width), ru, rd = shapes
    cols, ro = width // 2, rs // 4
    rows = [ro, ro + ru, ro + ru + rd]
    core = 1 - c if swapped else c
    first_x, first_y = jnp.where(core == 0, 1 - x, x), jnp.where(core == 0, y, 1 - y)
    second_x, second_y = jnp.where(core == 0, x, 1 - x), jnp.where(core == 0, 1 - y, y)
    mine, far = (x, y), (1 - x, 1 - y)
    first, second = (first_x, first_y), (second_x, second_y)
    if later:
        pieces = [(2, second), (3, second), (3, far)]
    else:
        pieces = [(k, who) for who in (mine, first, far) for k in (1, 2)]
        pieces += [(1, second), (3, mine), (3, first)]
    for at, (k, (px, py)) in enumerate(pieces):
        source = jnp.bitwise_xor(z, k)
        slot_row = k * rs
        p = 2 * px + py
        m = 2 * p + core
        piece = ref.at[at]
        copies.append(
            pltpu.make_async_copy(
                piece.at[pl.ds(0, ro)],
                out_all.at[
                    pl.ds(pl.multiple_of(slot_row + p * ro, 16), ro),
                    pl.ds(pl.multiple_of(core * cols, 128), cols),
                ],
                sems.at[0],
            )
        )
        copies.append(
            pltpu.make_async_copy(
                piece.at[pl.ds(rows[0], ru)],
                up_all.at[
                    pl.ds(pl.multiple_of(source * ru, 16), ru),
                    pl.ds(pl.multiple_of(m * cols, 128), cols),
                ],
                sems.at[1],
            )
        )
        for side in range(2):
            copies.append(
                pltpu.make_async_copy(
                    piece.at[pl.ds(rows[1 + side], rd)],
                    down_all.at[
                        pl.ds(pl.multiple_of((source * 8 + m) * rd, 16), rd),
                        pl.ds(side * cols, cols),
                    ],
                    sems.at[2],
                )
            )


def gather_kernel(out_w, up_w, down_w, early, early_swapped, late, *refs):
    out_all, up_all, down_all, sems = refs
    z = lax.axis_index("head")
    rs, ru, rd = out_w.shape[0], up_w.shape[0], down_w.shape[0]
    copies = [
        pltpu.make_async_copy(out_w, out_all.at[pl.ds(0, rs)], sems.at[0]),
        pltpu.make_async_copy(
            up_w, up_all.at[pl.ds(pl.multiple_of(z * ru, 16), ru)], sems.at[1]
        ),
        pltpu.make_async_copy(
            down_w, down_all.at[pl.ds(pl.multiple_of(z * rd, 16), rd)], sems.at[2]
        ),
    ]
    shapes = (out_w.shape, ru, rd // 8)
    laid(copies, early, False, False, shapes, refs[:3], sems)
    laid(copies, early_swapped, True, False, shapes, refs[:3], sems)
    laid(copies, late, False, True, shapes, refs[:3], sems)
    for copy in copies:
        copy.start()
    for copy in copies:
        copy.wait()


def gathered(out_weight, up_weight, down_weight, *held):
    width, hidden_units = up_weight.shape[0] * ZS, up_weight.shape[1]
    made = lambda *shape: jax.ShapeDtypeStruct(shape, jnp.bfloat16)
    return pl.pallas_call(
        gather_kernel,
        out_shape=[made(width, width), made(width, hidden_units), made(hidden_units, width)],
        in_specs=[ANY] * (3 + len(held)),
        out_specs=[VMEM] * 3,
        scratch_shapes=[pltpu.SemaphoreType.DMA((3,))],
        compiler_params=pltpu.CompilerParams(vmem_limit_bytes=20 * MIB),
        cost_estimate=pl.CostEstimate(flops=0, bytes_accessed=12 * MIB, transcendentals=0),
        name="gather",
    )(out_weight, up_weight, down_weight, *held)


def feed_kernel(gain, surface, *refs):
    ctx_slots, refs = refs[:ZS], refs[ZS + 3 :]
    late_swapped, o_ref, out_all, up_all, down_all, sems = refs
    width, hidden_units = up_all.shape
    copies = []
    shapes = ((width // ZS, width), width // ZS, hidden_units // ZS // 8)
    laid(copies, late_swapped, True, True, shapes, (out_all, up_all, down_all), sems)
    first = [copies[i] for i in range(len(copies)) if i % 4 == 0]
    second = [copies[i] for i in range(len(copies)) if i % 4 == 1]
    third = [copies[i] for i in range(len(copies)) if i % 4 > 1]
    for copy in first + second + third:
        copy.start()

    tiles = [ctx_slots[s][h] for s in range(ZS) for h in range(HZ)]
    low = lax.broadcasted_iota(jnp.int32, tiles[0].shape, 1) < HD
    upper, lower = [], []
    for left, right in zip(tiles[::2], tiles[1::2]):
        upper.append(jnp.where(low, left, pltpu.roll(right, HD, 1)))
        lower.append(jnp.where(low, pltpu.roll(left, HD, 1), right))
    context = jnp.concatenate(
        [jnp.concatenate(upper, axis=1), jnp.concatenate(lower, axis=1)], axis=0
    )
    for copy in first:
        copy.wait()
    hidden = surface[...].astype(jnp.float32) + jnp.dot(
        context, out_all[...], preferred_element_type=jnp.float32
    )
    mean_square = jnp.mean(hidden * hidden, axis=1, keepdims=True)
    normed = (hidden * lax.rsqrt(mean_square + 1e-05) * gain[...]).astype(jnp.bfloat16)
    for copy in second:
        copy.wait()
    total = hidden
    for step in range(hidden_units // width):
        pre = jnp.dot(
            normed, up_all[:, step * width : (step + 1) * width], preferred_element_type=jnp.float32
        )
        act = jax.nn.gelu(pre, approximate=True).astype(jnp.bfloat16)
        if step == 0:
            for copy in third:
                copy.wait()
        total = total + jnp.dot(
            act, down_all[step * width : (step + 1) * width, :], preferred_element_type=jnp.float32
        )
    o_ref[...] = total.astype(jnp.bfloat16)


def fed(gain, surface, ctx_slots, weights, late_swapped):
    outs = pl.pallas_call(
        feed_kernel,
        out_shape=[jax.ShapeDtypeStruct(v.shape, jnp.bfloat16) for v in (surface, *weights)],
        in_specs=[VMEM, VMEM] + [VMEM] * (ZS + 3) + [ANY],
        out_specs=[VMEM] * 4,
        scratch_shapes=[pltpu.SemaphoreType.DMA((3,))],
        input_output_aliases={2 + ZS: 1, 3 + ZS: 2, 4 + ZS: 3},
        compiler_params=pltpu.CompilerParams(vmem_limit_bytes=30 * MIB),
        cost_estimate=pl.CostEstimate(
            flops=3 * 10**9, bytes_accessed=12 * MIB, transcendentals=10**6
        ),
        name="feed",
    )(gain, surface, *ctx_slots, *weights, late_swapped)
    return outs[0]


def split_shards(
    queries,
    keys_values,
    surface,
    out_weight,
    up_weight,
    down_weight,
    norm_gain,
    block_lists,
    list_lengths,
):
    kv_slots, q_slots, piece = packed(
        block_lists, list_lengths, queries, keys_values, out_weight, up_weight, down_weight
    )
    kv_slots, q_slots = list(kv_slots), list(q_slots)
    near, q, far = {0: kv_slots[0]}, {0: q_slots[0]}, {}
    w12 = jnp.concatenate([sent(piece, across_head(k)) for k in (1, 2)])
    far[0] = sent(kv_slots[0], over_blk)
    near[1], near[3] = (sent(kv_slots[s], across_head(s)) for s in (1, 3))
    first12 = sent(w12, plane_first)
    far13 = sent(jnp.stack([near[1], near[3]]), over_blk)
    near[2] = sent(kv_slots[2], across_head(2))
    w3 = sent(w12[1:], across_head(1))
    near[2], w3, q_slots[1], q_slots[2], q_slots[3] = lax.optimization_barrier(
        (near[2], w3, q_slots[1], q_slots[2], q_slots[3])
    )
    far[2] = sent(near[2], over_blk)
    more12 = sent(jnp.concatenate([first12, w12[:1]]), plane_second)
    first12, far13, near[2], w3 = lax.optimization_barrier((first12, far13, near[2], w3))
    far[1], far[3] = far13[0], far13[1]
    away = (2, 1, 3)
    for s in away:
        q[s] = sent(q_slots[s], across_head(s))
    more3 = sent(first12[1:], across_head(1))
    blocks = jnp.stack([near[s] for s in range(ZS)] + [far[s] for s in range(ZS)])
    ctx_slots = dict(zip(away, attended(blocks, [q[s] for s in away])))
    more12, more3 = after(more12, ctx_slots[2]), after(more3, ctx_slots[2])
    early = jnp.concatenate([w12, first12, more12, w3, more3])
    late = sent(jnp.concatenate([w12[1:], w3, more3]), plane_second)
    for s in away:
        ctx_slots[s] = sent(ctx_slots[s], across_head(s))
    (ctx_slots[0],) = attended(blocks, [q[0]])
    early_swapped = sent(after(early, ctx_slots[0]), other_core)
    late = after(late, ctx_slots[0], ctx_slots[1], ctx_slots[2], ctx_slots[3])
    late_swapped = sent(late, other_core)
    whole = gathered(out_weight, up_weight, down_weight, early, early_swapped, late)
    ctx_slots = [ctx_slots[s] for s in range(ZS)]
    return fed(norm_gain[None, :], surface, ctx_slots, whole, late_swapped)


def solution(mesh):
    sizes = (mesh.shape["blk"], mesh.shape["head"], mesh.shape["bend"])
    if sizes == (2, 4, 4):
        mesh = Mesh(mesh.devices.reshape(SIZES), AXES)
        parts, shards = ("side", "core"), split_shards
    else:
        parts, shards = ("bend",), ring_shards
    rows = parts + ("blk", "head")
    return jax.shard_map(
        shards,
        mesh=mesh,
        in_specs=(
            P(rows, None),
            P(None, rows, None),
            P(rows, None),
            P("head", None),
            P("head", None),
            P("head", None),
            P(),
            P(rows, None),
            P(rows),
        ),
        out_specs=P(rows, None),
        check_vma=False,
    )
```

```python
import functools
import itertools

import jax
import jax.numpy as jnp
from jax import lax
from jax.experimental import pallas as pl
from jax.experimental.pallas import tpu as pltpu
from jax.sharding import Mesh
from jax.sharding import PartitionSpec as P

HEADS = 12
HD = 64
LIST = 4
MIB = 1024 * 1024
LOG2E = 1.4426950408889634


def passed_along(block, axis, distance):
    devices = range(lax.axis_size(axis))
    route = [((i - distance) % len(devices), i) for i in devices]
    return lax.ppermute(block, axis, route)


def fold_rows(running, left_side, portion):
    return running + jnp.dot(left_side, portion, preferred_element_type=jnp.float32)


def ring_shards(
    queries,
    keys_values,
    surface,
    out_weight,
    up_weight,
    down_weight,
    norm_gain,
    block_lists,
    list_lengths,
):
    row_count, feature_width = queries.shape
    query_blocks = block_lists.shape[0]
    block_rows = row_count // query_blocks
    loop_size = lax.axis_size(("blk", "head"))
    cycle_reach = min(3, (loop_size - 1) // 2)
    own_index = lax.axis_index(("blk", "head"))
    query_heads = queries.reshape(query_blocks, block_rows, HEADS, HD)
    score_scale = 1.0 / HD**0.5
    entry_live = jnp.arange(LIST, dtype=jnp.int32)[None, :] < list_lengths[:, None]
    start_state = (
        jnp.full((query_blocks, HEADS, block_rows), -1e30, jnp.float32),
        jnp.zeros((query_blocks, HEADS, block_rows), jnp.float32),
        jnp.zeros((query_blocks, HEADS, block_rows, HD), jnp.float32),
    )

    def absorb(softmax_state, anchor_pair, source):
        listed = jnp.any((block_lists == source) & entry_live, axis=1)
        running_max, running_sum, running_acc = softmax_state
        block_keys = anchor_pair[0].reshape(block_rows, HEADS, HD)
        block_values = anchor_pair[1].reshape(block_rows, HEADS, HD)
        scores = (
            jnp.einsum(
                "bqhd,khd->bhqk", query_heads, block_keys, preferred_element_type=jnp.float32
            )
            * score_scale
        )
        block_max = jnp.max(scores, axis=3)
        new_max = jnp.where(listed[:, None, None], jnp.maximum(running_max, block_max), running_max)
        ratio = jnp.exp(running_max - new_max)
        weights_exp = jnp.where(
            listed[:, None, None, None], jnp.exp(scores - new_max[..., None]), 0.0
        )
        new_sum = running_sum * ratio + jnp.sum(weights_exp, axis=3)
        probs = weights_exp.astype(jnp.bfloat16)
        new_acc = running_acc * ratio[..., None] + jnp.einsum(
            "bhqk,khd->bhqd", probs, block_values, preferred_element_type=jnp.float32
        )
        return (new_max, new_sum, new_acc)

    moving = passed_along(keys_values, ("blk", "head"), -cycle_reach)
    source = (own_index + cycle_reach) % loop_size
    softmax_state = absorb(start_state, moving, source)
    for cycle_turn in range(2 * cycle_reach):
        moving = passed_along(moving, ("blk", "head"), 1)
        source = (source - 1) % loop_size
        softmax_state = absorb(softmax_state, moving, source)
    final_max, final_sum, final_acc = softmax_state
    context = final_acc / final_sum[..., None]
    context = (
        jnp.transpose(context, (0, 2, 1, 3)).reshape(row_count, feature_width).astype(jnp.bfloat16)
    )
    residual = surface.astype(jnp.float32)
    hidden = fold_rows(residual, context, lax.all_gather(out_weight, "head", axis=0, tiled=True))
    mean_square = jnp.mean(hidden * hidden, axis=1, keepdims=True)
    normed = (hidden * lax.rsqrt(mean_square + 1e-05) * norm_gain[None, :]).astype(jnp.bfloat16)
    up_start = jnp.zeros((row_count, up_weight.shape[1]), jnp.float32)
    pre_gelu = fold_rows(up_start, normed, lax.all_gather(up_weight, "head", axis=0, tiled=True))
    activated = jax.nn.gelu(pre_gelu, approximate=True).astype(jnp.bfloat16)
    mixed_out = fold_rows(
        hidden, activated, lax.all_gather(down_weight, "head", axis=0, tiled=True)
    )
    return mixed_out.astype(jnp.bfloat16)


AXES = ("blk", "head", "side", "core")
SIZES = (2, 4, 2, 2)
DEVICES = list(itertools.product(*(range(size) for size in SIZES)))
ZS = 4
HZ = HEADS // ZS
NOTE = 16
ANY = pl.BlockSpec(memory_space=pl.ANY)
SMEM = pl.BlockSpec(memory_space=pltpu.SMEM)
VMEM = pl.BlockSpec(memory_space=pltpu.VMEM)
HBM = pl.BlockSpec(memory_space=pltpu.HBM)


def flat(x, z, y, c):
    return ((x * SIZES[1] + z) * SIZES[2] + y) * SIZES[3] + c


def sent(value, route):
    return lax.ppermute(value, AXES, [(flat(*d), flat(*route(*d))) for d in DEVICES])


def across_head(slot):
    return lambda x, z, y, c: (x, z ^ slot, y, c)


def over_blk(x, z, y, c):
    return (1 - x, z, y, c)


def plane_first(x, z, y, c):
    return (1 - x, z, y, c) if c == 0 else (x, z, 1 - y, c)


def plane_second(x, z, y, c):
    return (x, z, 1 - y, c) if c == 0 else (1 - x, z, y, c)


def other_core(x, z, y, c):
    return (x, z, y, 1 - c)


def after(value, *earlier):
    return lax.optimization_barrier((value,) + earlier)[0]


def pack_kernel(listed_hbm, length_hbm, q_hbm, kv_hbm, out_w, up_w, down_w, *refs):
    kv_slots, q_slots, piece = refs[:ZS], refs[ZS : 2 * ZS], refs[2 * ZS]
    kv_all, q_all, q_ref, kv_ref, listed, length, sems = refs[2 * ZS + 1 :]
    x, z, y, c = (lax.axis_index(axis) for axis in AXES)
    p = 2 * x + y
    m = 2 * p + c
    ro, cols = out_w.shape[0] // 4, out_w.shape[1] // 2
    ru, rd = up_w.shape[0], down_w.shape[0] // 8
    rows = [ro, ro + ru, ro + ru + rd]
    copies = [
        pltpu.make_async_copy(kv_hbm, kv_ref, sems.at[0]),
        pltpu.make_async_copy(q_hbm, q_ref, sems.at[1]),
        pltpu.make_async_copy(listed_hbm, listed, sems.at[3]),
        pltpu.make_async_copy(length_hbm, length, sems.at[4]),
    ]
    copies += [
        pltpu.make_async_copy(
            out_w.at[pl.ds(pl.multiple_of(p * ro, 16), ro), pl.ds(pl.multiple_of(c * cols, 128), cols)],
            piece.at[0, pl.ds(0, ro)],
            sems.at[2],
        ),
        pltpu.make_async_copy(
            up_w.at[:, pl.ds(pl.multiple_of(m * cols, 128), cols)],
            piece.at[0, pl.ds(rows[0], ru)],
            sems.at[2],
        ),
    ]
    for side in range(2):
        copies.append(
            pltpu.make_async_copy(
                down_w.at[pl.ds(pl.multiple_of(m * rd, 16), rd), pl.ds(side * cols, cols)],
                piece.at[0, pl.ds(rows[1 + side], rd)],
                sems.at[2],
            )
        )
    for copy in copies:
        copy.start()
    n = q_ref.shape[0] // 2
    copies[0].wait()
    for pair in range(HEADS // 2):
        lanes = slice(pair * 2 * HD, (pair + 1) * 2 * HD)
        keys, values = kv_ref[0, :, lanes], kv_ref[1, :, lanes]
        even, odd = 2 * pair, 2 * pair + 1
        low = lax.broadcasted_iota(jnp.int32, keys.shape, 1) < HD
        kv_all[even // HZ, even % HZ] = jnp.where(low, keys, pltpu.roll(values, HD, 1))
        kv_all[odd // HZ, odd % HZ] = jnp.where(low, pltpu.roll(keys, HD, 1), values)
    copies[1].wait()
    for pair in range(HEADS // 2):
        lanes = slice(pair * 2 * HD, (pair + 1) * 2 * HD)
        upper, lower = q_ref[:n, lanes], q_ref[n:, lanes]
        even, odd = 2 * pair, 2 * pair + 1
        low = lax.broadcasted_iota(jnp.int32, upper.shape, 1) < HD
        q_all[even // HZ, (even % HZ) * n : (even % HZ + 1) * n] = jnp.where(
            low, upper, pltpu.roll(lower, HD, 1)
        )
        q_all[odd // HZ, (odd % HZ) * n : (odd % HZ + 1) * n] = jnp.where(
            low, pltpu.roll(upper, HD, 1), lower
        )
    copies[2].wait()
    copies[3].wait()
    lane = lax.broadcasted_iota(jnp.int32, (NOTE, 2 * HD), 1)
    note = jnp.where(lane == LIST, length[0], 0)
    for j in range(LIST):
        note = jnp.where(lane == j, listed[0, j], note)
    note = note.astype(jnp.float32).astype(jnp.bfloat16)
    for s in range(ZS):
        there = jnp.bitwise_xor(z, s)
        kv_slots[s][...] = kv_all[there]
        q_slots[s][: HZ * n] = q_all[there]
        q_slots[s][HZ * n :] = note
    for copy in copies[4:]:
        copy.wait()


def packed(listed, length, queries, keys_values, out_weight, up_weight, down_weight):
    rows, width = queries.shape
    cols = width // 2
    piece_rows = out_weight.shape[0] // 4 + up_weight.shape[0] + down_weight.shape[0] // 4
    kv_shape, q_rows = (HZ, rows, 2 * HD), HZ * rows // 2
    made = lambda shape: jax.ShapeDtypeStruct(shape, jnp.bfloat16)
    outs = pl.pallas_call(
        pack_kernel,
        out_shape=[made(kv_shape)] * ZS + [made((q_rows + NOTE, 2 * HD))] * ZS + [made((1, piece_rows, cols))],
        in_specs=[HBM] * 7,
        out_specs=[VMEM] * (2 * ZS + 1),
        scratch_shapes=[
            pltpu.VMEM((ZS,) + kv_shape, jnp.bfloat16),
            pltpu.VMEM((ZS, q_rows, 2 * HD), jnp.bfloat16),
            pltpu.VMEM(queries.shape, jnp.bfloat16),
            pltpu.VMEM(keys_values.shape, jnp.bfloat16),
            pltpu.SMEM(listed.shape, jnp.int32),
            pltpu.SMEM(length.shape, jnp.int32),
            pltpu.SemaphoreType.DMA((5,)),
        ],
        compiler_params=pltpu.CompilerParams(vmem_limit_bytes=55 * MIB),
        cost_estimate=pl.CostEstimate(flops=0, bytes_accessed=4 * MIB, transcendentals=0),
        name="pack_heads",
    )(listed, length, queries, keys_values, out_weight, up_weight, down_weight)
    return outs[:ZS], outs[ZS : 2 * ZS], outs[2 * ZS]


def attend_kernel(blocks, *refs):
    q_refs, o_refs = refs[: len(refs) // 2], refs[len(refs) // 2 :]
    x, z = (lax.axis_index(axis) for axis in AXES[:2])
    n = o_refs[0].shape[1]
    low = lax.broadcasted_iota(jnp.int32, (n, 2 * HD), 1) < HD
    key_lanes = lax.broadcasted_iota(jnp.int32, (2 * n, 2 * HD), 1) < HD
    scale = LOG2E / HD**0.5
    row = lax.broadcasted_iota(jnp.int32, (NOTE, 2 * HD), 0)
    lane = lax.broadcasted_iota(jnp.int32, (NOTE, 2 * HD), 1)
    digit = jnp.left_shift(1, 3 * jnp.minimum(lane, LIST))
    digit = jnp.where((row == 0) & (lane <= LIST), digit, 0).astype(jnp.float32)
    codes = [
        jnp.sum(q_ref[HZ * n :].astype(jnp.float32) * digit).astype(jnp.int32) for q_ref in q_refs
    ]
    for q_ref, o_ref, code in zip(q_refs, o_refs, codes):
        at = []
        for j in range(LIST):
            block = jnp.bitwise_and(jnp.right_shift(code, 3 * j), 7)
            side, source = block // ZS, lax.rem(block, ZS)
            at.append(jnp.where(side == x, 0, ZS) + jnp.bitwise_xor(z, source))
        length = jnp.right_shift(code, 3 * LIST)

        def scored(h, count, q_ref=q_ref, at=at):
            pair = q_ref[h * n : (h + 1) * n]
            none = jnp.zeros_like(pair)
            q = jnp.concatenate(
                [jnp.where(low, pair, none), jnp.where(low, pltpu.roll(pair, HD, 1), none)], axis=0
            )
            scores = [
                lax.dot_general(
                    q, blocks[at[j], h], (((1,), (1,)), ((), ())), preferred_element_type=jnp.float32
                )
                for j in range(count)
            ]
            return scores, jnp.max(functools.reduce(jnp.maximum, scores), axis=1, keepdims=True)

        def summed(h, count, scores, top, o_ref=o_ref, at=at):
            acc = None
            for j in range(count):
                weights = jnp.exp2((scores[j] - top) * scale).astype(jnp.bfloat16)
                values = blocks[at[j], h]
                values = jnp.where(key_lanes, jnp.ones_like(values), values)
                part = jnp.dot(weights, values, preferred_element_type=jnp.float32)
                acc = part if j == 0 else acc + part
            result = acc / pltpu.roll(acc, HD, 1)
            upper, lower = result[:n], result[n:]
            o_ref[h] = jnp.where(low, pltpu.roll(upper, HD, 1), lower).astype(jnp.bfloat16)

        for count in range(1, LIST + 1):

            @pl.when(length == count)
            def _(count=count, scored=scored, summed=summed):
                held = [scored(h, count) for h in range(HZ)]
                for h in range(HZ):
                    summed(h, count, *held[h])


def attended(blocks, queries):
    made = jax.ShapeDtypeStruct((HZ, blocks.shape[2] // 2, 2 * HD), jnp.bfloat16)
    return pl.pallas_call(
        attend_kernel,
        out_shape=[made] * len(queries),
        in_specs=[VMEM] * (1 + len(queries)),
        out_specs=[VMEM] * len(queries),
        compiler_params=pltpu.CompilerParams(vmem_limit_bytes=16 * MIB),
        cost_estimate=pl.CostEstimate(
            flops=5 * 10**8, bytes_accessed=MIB, transcendentals=8 * 10**5
        ),
        name="attend",
    )(blocks, *queries)


def laid(copies, ref, swapped, later, shapes, into, sems):
    x, z, y, c = (lax.axis_index(axis) for axis in AXES)
    out_all, up_all, down_all = into
    (rs, width), ru, rd = shapes
    cols, ro = width // 2, rs // 4
    rows = [ro, ro + ru, ro + ru + rd]
    core = 1 - c if swapped else c
    first_x, first_y = jnp.where(core == 0, 1 - x, x), jnp.where(core == 0, y, 1 - y)
    second_x, second_y = jnp.where(core == 0, x, 1 - x), jnp.where(core == 0, 1 - y, y)
    mine, far = (x, y), (1 - x, 1 - y)
    first, second = (first_x, first_y), (second_x, second_y)
    if later:
        pieces = [(2, second), (3, second), (3, far)]
    else:
        pieces = [(k, who) for who in (mine, first, far) for k in (1, 2)]
        pieces += [(1, second), (3, mine), (3, first)]
    for at, (k, (px, py)) in enumerate(pieces):
        source = jnp.bitwise_xor(z, k)
        slot_row = k * rs
        p = 2 * px + py
        m = 2 * p + core
        piece = ref.at[at]
        copies.append(
            pltpu.make_async_copy(
                piece.at[pl.ds(0, ro)],
                out_all.at[
                    pl.ds(pl.multiple_of(slot_row + p * ro, 16), ro),
                    pl.ds(pl.multiple_of(core * cols, 128), cols),
                ],
                sems.at[0],
            )
        )
        copies.append(
            pltpu.make_async_copy(
                piece.at[pl.ds(rows[0], ru)],
                up_all.at[
                    pl.ds(pl.multiple_of(source * ru, 16), ru),
                    pl.ds(pl.multiple_of(m * cols, 128), cols),
                ],
                sems.at[1],
            )
        )
        for side in range(2):
            copies.append(
                pltpu.make_async_copy(
                    piece.at[pl.ds(rows[1 + side], rd)],
                    down_all.at[
                        pl.ds(pl.multiple_of((source * 8 + m) * rd, 16), rd),
                        pl.ds(side * cols, cols),
                    ],
                    sems.at[2],
                )
            )


def gather_kernel(out_w, up_w, down_w, early, early_swapped, late, *refs):
    out_all, up_all, down_all, sems = refs
    z = lax.axis_index("head")
    rs, ru, rd = out_w.shape[0], up_w.shape[0], down_w.shape[0]
    copies = [
        pltpu.make_async_copy(out_w, out_all.at[pl.ds(0, rs)], sems.at[0]),
        pltpu.make_async_copy(
            up_w, up_all.at[pl.ds(pl.multiple_of(z * ru, 16), ru)], sems.at[1]
        ),
        pltpu.make_async_copy(
            down_w, down_all.at[pl.ds(pl.multiple_of(z * rd, 16), rd)], sems.at[2]
        ),
    ]
    shapes = (out_w.shape, ru, rd // 8)
    laid(copies, early, False, False, shapes, refs[:3], sems)
    laid(copies, early_swapped, True, False, shapes, refs[:3], sems)
    laid(copies, late, False, True, shapes, refs[:3], sems)
    for copy in copies:
        copy.start()
    for copy in copies:
        copy.wait()


def gathered(out_weight, up_weight, down_weight, *held):
    width, hidden_units = up_weight.shape[0] * ZS, up_weight.shape[1]
    made = lambda *shape: jax.ShapeDtypeStruct(shape, jnp.bfloat16)
    return pl.pallas_call(
        gather_kernel,
        out_shape=[made(width, width), made(width, hidden_units), made(hidden_units, width)],
        in_specs=[ANY] * (3 + len(held)),
        out_specs=[VMEM] * 3,
        scratch_shapes=[pltpu.SemaphoreType.DMA((3,))],
        compiler_params=pltpu.CompilerParams(vmem_limit_bytes=20 * MIB),
        cost_estimate=pl.CostEstimate(flops=0, bytes_accessed=12 * MIB, transcendentals=0),
        name="gather",
    )(out_weight, up_weight, down_weight, *held)


def feed_kernel(gain, surface, *refs):
    ctx_slots, refs = refs[:ZS], refs[ZS + 3 :]
    late_swapped, o_ref, out_all, up_all, down_all, sems = refs
    width, hidden_units = up_all.shape
    copies = []
    shapes = ((width // ZS, width), width // ZS, hidden_units // ZS // 8)
    laid(copies, late_swapped, True, True, shapes, (out_all, up_all, down_all), sems)
    first = [copies[i] for i in range(len(copies)) if i % 4 == 0]
    second = [copies[i] for i in range(len(copies)) if i % 4 == 1]
    third = [copies[i] for i in range(len(copies)) if i % 4 > 1]
    for copy in first + second + third:
        copy.start()

    tiles = [ctx_slots[s][h] for s in range(ZS) for h in range(HZ)]
    low = lax.broadcasted_iota(jnp.int32, tiles[0].shape, 1) < HD
    upper, lower = [], []
    for left, right in zip(tiles[::2], tiles[1::2]):
        upper.append(jnp.where(low, left, pltpu.roll(right, HD, 1)))
        lower.append(jnp.where(low, pltpu.roll(left, HD, 1), right))
    context = jnp.concatenate(
        [jnp.concatenate(upper, axis=1), jnp.concatenate(lower, axis=1)], axis=0
    )
    for copy in first:
        copy.wait()
    hidden = surface[...].astype(jnp.float32) + jnp.dot(
        context, out_all[...], preferred_element_type=jnp.float32
    )
    mean_square = jnp.mean(hidden * hidden, axis=1, keepdims=True)
    normed = (hidden * lax.rsqrt(mean_square + 1e-05) * gain[...]).astype(jnp.bfloat16)
    for copy in second:
        copy.wait()
    total = hidden
    for step in range(hidden_units // width):
        pre = jnp.dot(
            normed, up_all[:, step * width : (step + 1) * width], preferred_element_type=jnp.float32
        )
        act = jax.nn.gelu(pre, approximate=True).astype(jnp.bfloat16)
        if step == 0:
            for copy in third:
                copy.wait()
        total = total + jnp.dot(
            act, down_all[step * width : (step + 1) * width, :], preferred_element_type=jnp.float32
        )
    o_ref[...] = total.astype(jnp.bfloat16)


def fed(gain, surface, ctx_slots, weights, late_swapped):
    outs = pl.pallas_call(
        feed_kernel,
        out_shape=[jax.ShapeDtypeStruct(v.shape, jnp.bfloat16) for v in (surface, *weights)],
        in_specs=[VMEM, VMEM] + [VMEM] * (ZS + 3) + [ANY],
        out_specs=[VMEM] * 4,
        scratch_shapes=[pltpu.SemaphoreType.DMA((3,))],
        input_output_aliases={2 + ZS: 1, 3 + ZS: 2, 4 + ZS: 3},
        compiler_params=pltpu.CompilerParams(vmem_limit_bytes=30 * MIB),
        cost_estimate=pl.CostEstimate(
            flops=3 * 10**9, bytes_accessed=12 * MIB, transcendentals=10**6
        ),
        name="feed",
    )(gain, surface, *ctx_slots, *weights, late_swapped)
    return outs[0]


def split_shards(
    queries,
    keys_values,
    surface,
    out_weight,
    up_weight,
    down_weight,
    norm_gain,
    block_lists,
    list_lengths,
):
    kv_slots, q_slots, piece = packed(
        block_lists, list_lengths, queries, keys_values, out_weight, up_weight, down_weight
    )
    kv_slots, q_slots = list(kv_slots), list(q_slots)
    near, q, far = {0: kv_slots[0]}, {0: q_slots[0]}, {}
    w12 = jnp.concatenate([sent(piece, across_head(k)) for k in (1, 2)])
    far[0] = sent(kv_slots[0], over_blk)
    near[1], near[3] = (sent(kv_slots[s], across_head(s)) for s in (1, 3))
    first12 = sent(w12, plane_first)
    far13 = sent(jnp.stack([near[1], near[3]]), over_blk)
    near[2] = sent(kv_slots[2], across_head(2))
    w3 = sent(w12[1:], across_head(1))
    near[2], w3, q_slots[1], q_slots[2], q_slots[3] = lax.optimization_barrier(
        (near[2], w3, q_slots[1], q_slots[2], q_slots[3])
    )
    far[2] = sent(near[2], over_blk)
    more12 = sent(jnp.concatenate([first12, w12[:1]]), plane_second)
    first12, far13, near[2], w3 = lax.optimization_barrier((first12, far13, near[2], w3))
    far[1], far[3] = far13[0], far13[1]
    away = (1, 3, 2)
    for s in away:
        q[s] = sent(q_slots[s], across_head(s))
    more3 = sent(first12[1:], across_head(1))
    blocks = jnp.stack([near[s] for s in range(ZS)] + [far[s] for s in range(ZS)])
    ctx_slots = dict(zip(away, attended(blocks, [q[s] for s in away])))
    more12, more3 = after(more12, ctx_slots[2]), after(more3, ctx_slots[2])
    early = jnp.concatenate([w12, first12, more12, w3, more3])
    late = sent(jnp.concatenate([w12[1:], w3, more3]), plane_second)
    for s in away:
        ctx_slots[s] = sent(ctx_slots[s], across_head(s))
    (ctx_slots[0],) = attended(blocks, [q[0]])
    early_swapped = sent(after(early, ctx_slots[0]), other_core)
    late = after(late, ctx_slots[0], ctx_slots[1], ctx_slots[2], ctx_slots[3])
    late_swapped = sent(late, other_core)
    whole = gathered(out_weight, up_weight, down_weight, early, early_swapped, late)
    ctx_slots = [ctx_slots[s] for s in range(ZS)]
    return fed(norm_gain[None, :], surface, ctx_slots, whole, late_swapped)


def solution(mesh):
    sizes = (mesh.shape["blk"], mesh.shape["head"], mesh.shape["bend"])
    if sizes == (2, 4, 4):
        mesh = Mesh(mesh.devices.reshape(SIZES), AXES)
        parts, shards = ("side", "core"), split_shards
    else:
        parts, shards = ("bend",), ring_shards
    rows = parts + ("blk", "head")
    return jax.shard_map(
        shards,
        mesh=mesh,
        in_specs=(
            P(rows, None),
            P(None, rows, None),
            P(rows, None),
            P("head", None),
            P("head", None),
            P("head", None),
            P(),
            P(rows, None),
            P(rows),
        ),
        out_specs=P(rows, None),
        check_vma=False,
    )
```

```python
import functools
import itertools

import jax
import jax.numpy as jnp
from jax import lax
from jax.experimental import pallas as pl
from jax.experimental.pallas import tpu as pltpu
from jax.sharding import Mesh
from jax.sharding import PartitionSpec as P

HEADS = 12
HD = 64
LIST = 4
MIB = 1024 * 1024
LOG2E = 1.4426950408889634


def passed_along(block, axis, distance):
    devices = range(lax.axis_size(axis))
    route = [((i - distance) % len(devices), i) for i in devices]
    return lax.ppermute(block, axis, route)


def fold_rows(running, left_side, portion):
    return running + jnp.dot(left_side, portion, preferred_element_type=jnp.float32)


def ring_shards(
    queries,
    keys_values,
    surface,
    out_weight,
    up_weight,
    down_weight,
    norm_gain,
    block_lists,
    list_lengths,
):
    row_count, feature_width = queries.shape
    query_blocks = block_lists.shape[0]
    block_rows = row_count // query_blocks
    loop_size = lax.axis_size(("blk", "head"))
    cycle_reach = min(3, (loop_size - 1) // 2)
    own_index = lax.axis_index(("blk", "head"))
    query_heads = queries.reshape(query_blocks, block_rows, HEADS, HD)
    score_scale = 1.0 / HD**0.5
    entry_live = jnp.arange(LIST, dtype=jnp.int32)[None, :] < list_lengths[:, None]
    start_state = (
        jnp.full((query_blocks, HEADS, block_rows), -1e30, jnp.float32),
        jnp.zeros((query_blocks, HEADS, block_rows), jnp.float32),
        jnp.zeros((query_blocks, HEADS, block_rows, HD), jnp.float32),
    )

    def absorb(softmax_state, anchor_pair, source):
        listed = jnp.any((block_lists == source) & entry_live, axis=1)
        running_max, running_sum, running_acc = softmax_state
        block_keys = anchor_pair[0].reshape(block_rows, HEADS, HD)
        block_values = anchor_pair[1].reshape(block_rows, HEADS, HD)
        scores = (
            jnp.einsum(
                "bqhd,khd->bhqk", query_heads, block_keys, preferred_element_type=jnp.float32
            )
            * score_scale
        )
        block_max = jnp.max(scores, axis=3)
        new_max = jnp.where(listed[:, None, None], jnp.maximum(running_max, block_max), running_max)
        ratio = jnp.exp(running_max - new_max)
        weights_exp = jnp.where(
            listed[:, None, None, None], jnp.exp(scores - new_max[..., None]), 0.0
        )
        new_sum = running_sum * ratio + jnp.sum(weights_exp, axis=3)
        probs = weights_exp.astype(jnp.bfloat16)
        new_acc = running_acc * ratio[..., None] + jnp.einsum(
            "bhqk,khd->bhqd", probs, block_values, preferred_element_type=jnp.float32
        )
        return (new_max, new_sum, new_acc)

    moving = passed_along(keys_values, ("blk", "head"), -cycle_reach)
    source = (own_index + cycle_reach) % loop_size
    softmax_state = absorb(start_state, moving, source)
    for cycle_turn in range(2 * cycle_reach):
        moving = passed_along(moving, ("blk", "head"), 1)
        source = (source - 1) % loop_size
        softmax_state = absorb(softmax_state, moving, source)
    final_max, final_sum, final_acc = softmax_state
    context = final_acc / final_sum[..., None]
    context = (
        jnp.transpose(context, (0, 2, 1, 3)).reshape(row_count, feature_width).astype(jnp.bfloat16)
    )
    residual = surface.astype(jnp.float32)
    hidden = fold_rows(residual, context, lax.all_gather(out_weight, "head", axis=0, tiled=True))
    mean_square = jnp.mean(hidden * hidden, axis=1, keepdims=True)
    normed = (hidden * lax.rsqrt(mean_square + 1e-05) * norm_gain[None, :]).astype(jnp.bfloat16)
    up_start = jnp.zeros((row_count, up_weight.shape[1]), jnp.float32)
    pre_gelu = fold_rows(up_start, normed, lax.all_gather(up_weight, "head", axis=0, tiled=True))
    activated = jax.nn.gelu(pre_gelu, approximate=True).astype(jnp.bfloat16)
    mixed_out = fold_rows(
        hidden, activated, lax.all_gather(down_weight, "head", axis=0, tiled=True)
    )
    return mixed_out.astype(jnp.bfloat16)


AXES = ("blk", "head", "side", "core")
SIZES = (2, 4, 2, 2)
DEVICES = list(itertools.product(*(range(size) for size in SIZES)))
ZS = 4
HZ = HEADS // ZS
NOTE = 16
ANY = pl.BlockSpec(memory_space=pl.ANY)
SMEM = pl.BlockSpec(memory_space=pltpu.SMEM)
VMEM = pl.BlockSpec(memory_space=pltpu.VMEM)
HBM = pl.BlockSpec(memory_space=pltpu.HBM)


def flat(x, z, y, c):
    return ((x * SIZES[1] + z) * SIZES[2] + y) * SIZES[3] + c


def sent(value, route):
    return lax.ppermute(value, AXES, [(flat(*d), flat(*route(*d))) for d in DEVICES])


def across_head(slot):
    return lambda x, z, y, c: (x, z ^ slot, y, c)


def over_blk(x, z, y, c):
    return (1 - x, z, y, c)


def plane_first(x, z, y, c):
    return (1 - x, z, y, c) if c == 0 else (x, z, 1 - y, c)


def plane_second(x, z, y, c):
    return (x, z, 1 - y, c) if c == 0 else (1 - x, z, y, c)


def other_core(x, z, y, c):
    return (x, z, y, 1 - c)


def after(value, *earlier):
    return lax.optimization_barrier((value,) + earlier)[0]


def cut_kernel(out_w, up_w, down_w, piece, sem):
    x, z, y, c = (lax.axis_index(axis) for axis in AXES)
    p = 2 * x + y
    m = 2 * p + c
    ro, cols = out_w.shape[0] // 4, out_w.shape[1] // 2
    ru, rd = up_w.shape[0], down_w.shape[0] // 8
    rows = [ro, ro + ru, ro + ru + rd]
    copies = []
    copies += [
        pltpu.make_async_copy(
            out_w.at[pl.ds(pl.multiple_of(p * ro, 16), ro), pl.ds(pl.multiple_of(c * cols, 128), cols)],
            piece.at[0, pl.ds(0, ro)],
            sem.at[0],
        ),
        pltpu.make_async_copy(
            up_w.at[:, pl.ds(pl.multiple_of(m * cols, 128), cols)],
            piece.at[0, pl.ds(rows[0], ru)],
            sem.at[0],
        ),
    ]
    for side in range(2):
        copies.append(
            pltpu.make_async_copy(
                down_w.at[pl.ds(pl.multiple_of(m * rd, 16), rd), pl.ds(side * cols, cols)],
                piece.at[0, pl.ds(rows[1 + side], rd)],
                sem.at[0],
            )
        )
    for copy in copies:
        copy.start()
    for copy in copies:
        copy.wait()


def cut_piece(out_weight, up_weight, down_weight):
    rows = out_weight.shape[0] // 4 + up_weight.shape[0] + down_weight.shape[0] // 4
    return pl.pallas_call(
        cut_kernel,
        out_shape=jax.ShapeDtypeStruct((1, rows, out_weight.shape[1] // 2), jnp.bfloat16),
        in_specs=[HBM] * 3,
        out_specs=VMEM,
        scratch_shapes=[pltpu.SemaphoreType.DMA((1,))],
        compiler_params=pltpu.CompilerParams(vmem_limit_bytes=58 * MIB),
        cost_estimate=pl.CostEstimate(flops=0, bytes_accessed=MIB, transcendentals=0),
        name="cut_piece",
    )(out_weight, up_weight, down_weight)


def pack_kernel(listed_hbm, length_hbm, q_hbm, kv_hbm, *refs):
    kv_slots, q_slots = refs[:ZS], refs[ZS : 2 * ZS]
    kv_all, q_all, q_ref, kv_ref, listed, length, sems = refs[2 * ZS :]
    z = lax.axis_index("head")
    copies = [
        pltpu.make_async_copy(kv_hbm, kv_ref, sems.at[0]),
        pltpu.make_async_copy(q_hbm, q_ref, sems.at[1]),
        pltpu.make_async_copy(listed_hbm, listed, sems.at[3]),
        pltpu.make_async_copy(length_hbm, length, sems.at[4]),
    ]
    for copy in copies:
        copy.start()
    n = q_ref.shape[0] // 2
    copies[0].wait()
    for pair in range(HEADS // 2):
        lanes = slice(pair * 2 * HD, (pair + 1) * 2 * HD)
        keys, values = kv_ref[0, :, lanes], kv_ref[1, :, lanes]
        even, odd = 2 * pair, 2 * pair + 1
        low = lax.broadcasted_iota(jnp.int32, keys.shape, 1) < HD
        kv_all[even // HZ, even % HZ] = jnp.where(low, keys, pltpu.roll(values, HD, 1))
        kv_all[odd // HZ, odd % HZ] = jnp.where(low, pltpu.roll(keys, HD, 1), values)
    copies[1].wait()
    for pair in range(HEADS // 2):
        lanes = slice(pair * 2 * HD, (pair + 1) * 2 * HD)
        upper, lower = q_ref[:n, lanes], q_ref[n:, lanes]
        even, odd = 2 * pair, 2 * pair + 1
        low = lax.broadcasted_iota(jnp.int32, upper.shape, 1) < HD
        q_all[even // HZ, (even % HZ) * n : (even % HZ + 1) * n] = jnp.where(
            low, upper, pltpu.roll(lower, HD, 1)
        )
        q_all[odd // HZ, (odd % HZ) * n : (odd % HZ + 1) * n] = jnp.where(
            low, pltpu.roll(upper, HD, 1), lower
        )
    copies[2].wait()
    copies[3].wait()
    lane = lax.broadcasted_iota(jnp.int32, (NOTE, 2 * HD), 1)
    note = jnp.where(lane == LIST, length[0], 0)
    for j in range(LIST):
        note = jnp.where(lane == j, listed[0, j], note)
    note = note.astype(jnp.float32).astype(jnp.bfloat16)
    for s in range(ZS):
        there = jnp.bitwise_xor(z, s)
        kv_slots[s][...] = kv_all[there]
        q_slots[s][: HZ * n] = q_all[there]
        q_slots[s][HZ * n :] = note


def packed(listed, length, queries, keys_values):
    rows = queries.shape[0]
    kv_shape, q_rows = (HZ, rows, 2 * HD), HZ * rows // 2
    made = lambda shape: jax.ShapeDtypeStruct(shape, jnp.bfloat16)
    outs = pl.pallas_call(
        pack_kernel,
        out_shape=[made(kv_shape)] * ZS + [made((q_rows + NOTE, 2 * HD))] * ZS,
        in_specs=[HBM] * 4,
        out_specs=[VMEM] * (2 * ZS),
        scratch_shapes=[
            pltpu.VMEM((ZS,) + kv_shape, jnp.bfloat16),
            pltpu.VMEM((ZS, q_rows, 2 * HD), jnp.bfloat16),
            pltpu.VMEM(queries.shape, jnp.bfloat16),
            pltpu.VMEM(keys_values.shape, jnp.bfloat16),
            pltpu.SMEM(listed.shape, jnp.int32),
            pltpu.SMEM(length.shape, jnp.int32),
            pltpu.SemaphoreType.DMA((5,)),
        ],
        compiler_params=pltpu.CompilerParams(vmem_limit_bytes=55 * MIB),
        cost_estimate=pl.CostEstimate(flops=0, bytes_accessed=4 * MIB, transcendentals=0),
        name="pack_heads",
    )(listed, length, queries, keys_values)
    return outs[:ZS], outs[ZS:]


def attend_kernel(blocks, *refs):
    q_refs, o_refs = refs[: len(refs) // 2], refs[len(refs) // 2 :]
    x, z = (lax.axis_index(axis) for axis in AXES[:2])
    n = o_refs[0].shape[1]
    low = lax.broadcasted_iota(jnp.int32, (n, 2 * HD), 1) < HD
    key_lanes = lax.broadcasted_iota(jnp.int32, (2 * n, 2 * HD), 1) < HD
    scale = LOG2E / HD**0.5
    row = lax.broadcasted_iota(jnp.int32, (NOTE, 2 * HD), 0)
    lane = lax.broadcasted_iota(jnp.int32, (NOTE, 2 * HD), 1)
    digit = jnp.left_shift(1, 3 * jnp.minimum(lane, LIST))
    digit = jnp.where((row == 0) & (lane <= LIST), digit, 0).astype(jnp.float32)
    codes = [
        jnp.sum(q_ref[HZ * n :].astype(jnp.float32) * digit).astype(jnp.int32) for q_ref in q_refs
    ]
    for q_ref, o_ref, code in zip(q_refs, o_refs, codes):
        at = []
        for j in range(LIST):
            block = jnp.bitwise_and(jnp.right_shift(code, 3 * j), 7)
            side, source = block // ZS, lax.rem(block, ZS)
            at.append(jnp.where(side == x, 0, ZS) + jnp.bitwise_xor(z, source))
        length = jnp.right_shift(code, 3 * LIST)

        def scored(h, count, q_ref=q_ref, at=at):
            pair = q_ref[h * n : (h + 1) * n]
            none = jnp.zeros_like(pair)
            q = jnp.concatenate(
                [jnp.where(low, pair, none), jnp.where(low, pltpu.roll(pair, HD, 1), none)], axis=0
            )
            scores = [
                lax.dot_general(
                    q, blocks[at[j], h], (((1,), (1,)), ((), ())), preferred_element_type=jnp.float32
                )
                for j in range(count)
            ]
            return scores, jnp.max(functools.reduce(jnp.maximum, scores), axis=1, keepdims=True)

        def summed(h, count, scores, top, o_ref=o_ref, at=at):
            acc = None
            for j in range(count):
                weights = jnp.exp2((scores[j] - top) * scale).astype(jnp.bfloat16)
                values = blocks[at[j], h]
                values = jnp.where(key_lanes, jnp.ones_like(values), values)
                part = jnp.dot(weights, values, preferred_element_type=jnp.float32)
                acc = part if j == 0 else acc + part
            result = acc / pltpu.roll(acc, HD, 1)
            upper, lower = result[:n], result[n:]
            o_ref[h] = jnp.where(low, pltpu.roll(upper, HD, 1), lower).astype(jnp.bfloat16)

        for count in range(1, LIST + 1):

            @pl.when(length == count)
            def _(count=count, scored=scored, summed=summed):
                held = [scored(h, count) for h in range(HZ)]
                for h in range(HZ):
                    summed(h, count, *held[h])


def attended(blocks, queries):
    made = jax.ShapeDtypeStruct((HZ, blocks.shape[2] // 2, 2 * HD), jnp.bfloat16)
    return pl.pallas_call(
        attend_kernel,
        out_shape=[made] * len(queries),
        in_specs=[VMEM] * (1 + len(queries)),
        out_specs=[VMEM] * len(queries),
        compiler_params=pltpu.CompilerParams(vmem_limit_bytes=16 * MIB),
        cost_estimate=pl.CostEstimate(
            flops=5 * 10**8, bytes_accessed=MIB, transcendentals=8 * 10**5
        ),
        name="attend",
    )(blocks, *queries)


def laid(copies, ref, swapped, later, shapes, into, sems):
    x, z, y, c = (lax.axis_index(axis) for axis in AXES)
    out_all, up_all, down_all = into
    (rs, width), ru, rd = shapes
    cols, ro = width // 2, rs // 4
    rows = [ro, ro + ru, ro + ru + rd]
    core = 1 - c if swapped else c
    first_x, first_y = jnp.where(core == 0, 1 - x, x), jnp.where(core == 0, y, 1 - y)
    second_x, second_y = jnp.where(core == 0, x, 1 - x), jnp.where(core == 0, 1 - y, y)
    mine, far = (x, y), (1 - x, 1 - y)
    first, second = (first_x, first_y), (second_x, second_y)
    if later:
        pieces = [(2, second), (3, second), (3, far)]
    else:
        pieces = [(k, who) for who in (mine, first, far) for k in (1, 2)]
        pieces += [(1, second), (3, mine), (3, first)]
    for at, (k, (px, py)) in enumerate(pieces):
        source = jnp.bitwise_xor(z, k)
        slot_row = k * rs
        p = 2 * px + py
        m = 2 * p + core
        piece = ref.at[at]
        copies.append(
            pltpu.make_async_copy(
                piece.at[pl.ds(0, ro)],
                out_all.at[
                    pl.ds(pl.multiple_of(slot_row + p * ro, 16), ro),
                    pl.ds(pl.multiple_of(core * cols, 128), cols),
                ],
                sems.at[0],
            )
        )
        copies.append(
            pltpu.make_async_copy(
                piece.at[pl.ds(rows[0], ru)],
                up_all.at[
                    pl.ds(pl.multiple_of(source * ru, 16), ru),
                    pl.ds(pl.multiple_of(m * cols, 128), cols),
                ],
                sems.at[1],
            )
        )
        for side in range(2):
            copies.append(
                pltpu.make_async_copy(
                    piece.at[pl.ds(rows[1 + side], rd)],
                    down_all.at[
                        pl.ds(pl.multiple_of((source * 8 + m) * rd, 16), rd),
                        pl.ds(side * cols, cols),
                    ],
                    sems.at[2],
                )
            )


def gather_kernel(out_w, up_w, down_w, early, early_swapped, late, *refs):
    out_all, up_all, down_all, sems = refs
    z = lax.axis_index("head")
    rs, ru, rd = out_w.shape[0], up_w.shape[0], down_w.shape[0]
    copies = [
        pltpu.make_async_copy(out_w, out_all.at[pl.ds(0, rs)], sems.at[0]),
        pltpu.make_async_copy(
            up_w, up_all.at[pl.ds(pl.multiple_of(z * ru, 16), ru)], sems.at[1]
        ),
        pltpu.make_async_copy(
            down_w, down_all.at[pl.ds(pl.multiple_of(z * rd, 16), rd)], sems.at[2]
        ),
    ]
    shapes = (out_w.shape, ru, rd // 8)
    laid(copies, early, False, False, shapes, refs[:3], sems)
    laid(copies, early_swapped, True, False, shapes, refs[:3], sems)
    laid(copies, late, False, True, shapes, refs[:3], sems)
    for copy in copies:
        copy.start()
    for copy in copies:
        copy.wait()


def gathered(out_weight, up_weight, down_weight, *held):
    width, hidden_units = up_weight.shape[0] * ZS, up_weight.shape[1]
    made = lambda *shape: jax.ShapeDtypeStruct(shape, jnp.bfloat16)
    return pl.pallas_call(
        gather_kernel,
        out_shape=[made(width, width), made(width, hidden_units), made(hidden_units, width)],
        in_specs=[ANY] * (3 + len(held)),
        out_specs=[VMEM] * 3,
        scratch_shapes=[pltpu.SemaphoreType.DMA((3,))],
        compiler_params=pltpu.CompilerParams(vmem_limit_bytes=20 * MIB),
        cost_estimate=pl.CostEstimate(flops=0, bytes_accessed=12 * MIB, transcendentals=0),
        name="gather",
    )(out_weight, up_weight, down_weight, *held)


def feed_kernel(gain, surface, *refs):
    ctx_slots, refs = refs[:ZS], refs[ZS + 3 :]
    late_swapped, o_ref, out_all, up_all, down_all, sems = refs
    width, hidden_units = up_all.shape
    copies = []
    shapes = ((width // ZS, width), width // ZS, hidden_units // ZS // 8)
    laid(copies, late_swapped, True, True, shapes, (out_all, up_all, down_all), sems)
    first = [copies[i] for i in range(len(copies)) if i % 4 == 0]
    second = [copies[i] for i in range(len(copies)) if i % 4 == 1]
    third = [copies[i] for i in range(len(copies)) if i % 4 > 1]
    for copy in first + second + third:
        copy.start()

    tiles = [ctx_slots[s][h] for s in range(ZS) for h in range(HZ)]
    low = lax.broadcasted_iota(jnp.int32, tiles[0].shape, 1) < HD
    upper, lower = [], []
    for left, right in zip(tiles[::2], tiles[1::2]):
        upper.append(jnp.where(low, left, pltpu.roll(right, HD, 1)))
        lower.append(jnp.where(low, pltpu.roll(left, HD, 1), right))
    context = jnp.concatenate(
        [jnp.concatenate(upper, axis=1), jnp.concatenate(lower, axis=1)], axis=0
    )
    for copy in first:
        copy.wait()
    hidden = surface[...].astype(jnp.float32) + jnp.dot(
        context, out_all[...], preferred_element_type=jnp.float32
    )
    mean_square = jnp.mean(hidden * hidden, axis=1, keepdims=True)
    normed = (hidden * lax.rsqrt(mean_square + 1e-05) * gain[...]).astype(jnp.bfloat16)
    for copy in second:
        copy.wait()
    total = hidden
    for step in range(hidden_units // width):
        pre = jnp.dot(
            normed, up_all[:, step * width : (step + 1) * width], preferred_element_type=jnp.float32
        )
        act = jax.nn.gelu(pre, approximate=True).astype(jnp.bfloat16)
        if step == 0:
            for copy in third:
                copy.wait()
        total = total + jnp.dot(
            act, down_all[step * width : (step + 1) * width, :], preferred_element_type=jnp.float32
        )
    o_ref[...] = total.astype(jnp.bfloat16)


def fed(gain, surface, ctx_slots, weights, late_swapped):
    outs = pl.pallas_call(
        feed_kernel,
        out_shape=[jax.ShapeDtypeStruct(v.shape, jnp.bfloat16) for v in (surface, *weights)],
        in_specs=[VMEM, VMEM] + [VMEM] * (ZS + 3) + [ANY],
        out_specs=[VMEM] * 4,
        scratch_shapes=[pltpu.SemaphoreType.DMA((3,))],
        input_output_aliases={2 + ZS: 1, 3 + ZS: 2, 4 + ZS: 3},
        compiler_params=pltpu.CompilerParams(vmem_limit_bytes=30 * MIB),
        cost_estimate=pl.CostEstimate(
            flops=3 * 10**9, bytes_accessed=12 * MIB, transcendentals=10**6
        ),
        name="feed",
    )(gain, surface, *ctx_slots, *weights, late_swapped)
    return outs[0]


def split_shards(
    queries,
    keys_values,
    surface,
    out_weight,
    up_weight,
    down_weight,
    norm_gain,
    block_lists,
    list_lengths,
):
    piece = cut_piece(out_weight, up_weight, down_weight)
    kv_slots, q_slots = packed(block_lists, list_lengths, queries, keys_values)
    kv_slots, q_slots = list(kv_slots), list(q_slots)
    near, q, far = {0: kv_slots[0]}, {0: q_slots[0]}, {}
    w12 = jnp.concatenate([sent(piece, across_head(k)) for k in (1, 2)])
    far[0] = sent(kv_slots[0], over_blk)
    near[1], near[3] = (sent(kv_slots[s], across_head(s)) for s in (1, 3))
    first12 = sent(w12, plane_first)
    far13 = sent(jnp.stack([near[1], near[3]]), over_blk)
    near[2] = sent(kv_slots[2], across_head(2))
    w3 = sent(w12[1:], across_head(1))
    near[2], w3, q_slots[1], q_slots[2], q_slots[3] = lax.optimization_barrier(
        (near[2], w3, q_slots[1], q_slots[2], q_slots[3])
    )
    far[2] = sent(near[2], over_blk)
    more12 = sent(jnp.concatenate([first12, w12[:1]]), plane_second)
    first12, far13, near[2], w3 = lax.optimization_barrier((first12, far13, near[2], w3))
    far[1], far[3] = far13[0], far13[1]
    away = (1, 3, 2)
    for s in away:
        q[s] = sent(q_slots[s], across_head(s))
    more3 = sent(first12[1:], across_head(1))
    blocks = jnp.stack([near[s] for s in range(ZS)] + [far[s] for s in range(ZS)])
    ctx_slots = dict(zip(away, attended(blocks, [q[s] for s in away])))
    more12, more3 = after(more12, ctx_slots[2]), after(more3, ctx_slots[2])
    early = jnp.concatenate([w12, first12, more12, w3, more3])
    late = sent(jnp.concatenate([w12[1:], w3, more3]), plane_second)
    for s in away:
        ctx_slots[s] = sent(ctx_slots[s], across_head(s))
    (ctx_slots[0],) = attended(blocks, [q[0]])
    early_swapped = sent(after(early, ctx_slots[0]), other_core)
    late = after(late, ctx_slots[0], ctx_slots[1], ctx_slots[2], ctx_slots[3])
    late_swapped = sent(late, other_core)
    whole = gathered(out_weight, up_weight, down_weight, early, early_swapped, late)
    ctx_slots = [ctx_slots[s] for s in range(ZS)]
    return fed(norm_gain[None, :], surface, ctx_slots, whole, late_swapped)


def solution(mesh):
    sizes = (mesh.shape["blk"], mesh.shape["head"], mesh.shape["bend"])
    if sizes == (2, 4, 4):
        mesh = Mesh(mesh.devices.reshape(SIZES), AXES)
        parts, shards = ("side", "core"), split_shards
    else:
        parts, shards = ("bend",), ring_shards
    rows = parts + ("blk", "head")
    return jax.shard_map(
        shards,
        mesh=mesh,
        in_specs=(
            P(rows, None),
            P(None, rows, None),
            P(rows, None),
            P("head", None),
            P("head", None),
            P("head", None),
            P(),
            P(rows, None),
            P(rows),
        ),
        out_specs=P(rows, None),
        check_vma=False,
    )
```
